256 devices in a mesh: inst: 16 (over z, core), tp: 16 (over y, x).
Axes of the slice: x: 4, y: 4, z: 8, core: 2. Of those that a mesh axis runs over, the one named last changes fastest.
Arguments:
- queries: bfloat16 [3, 128, 8192], P(None, 'inst', 'tp'), may hold values from -8 to 8
- new_kv: bfloat16 [3, 128, 2, 1024], P(None, 'inst'), may hold values from -5 to 5
- page_cache: bfloat16 [2048, 2, 256, 1024], P('inst', None, 'tp'), may hold values from -6 to 6
- range_owner: int32 [16, 16], replicated, may hold values from 0 to 127, as said below
- range_start: int32 [16, 16], replicated, may hold values from 0 to 127, as said below
- range_tokens: int32 [16, 16], replicated, may hold values from 1 to 28928, as said below
Outputs:
- attention: bfloat16 [3, 128, 8192], P(None, 'inst', 'tp')
The draws below stay inside these ranges and needn't reach their ends.
Inputs may be any that keep to these rules, and one draw needn't show every extreme that they name: `range_owner`: every request is homed at instance request // 8. Of the ranges one instance lends, at most 2 belong to requests of one home instance; in every draw one home instance receives exactly 2 ranges from every lender. `range_start`: the ranges of one lender tile its pool without gaps, in order of k: the first starts at page 0 and each next one starts where the previous one's pages end. `range_tokens`: A range of c pages holds more than 256 * (c - 1) positions.
All inputs are finite; a program needn't handle non-finite values.
Results may differ from the reference program's by a relative error of at most 0.003.
Values may be sent and summed in bfloat16 or wider, within the bound.
No kernel may reach another device: no remote copies, remote signals or barrier semaphores. Data moves between devices by JAX's collectives and lax.ppermute only.
A program may use at most 128 MiB of HBM per device.

```python
import math
import jax
import jax.numpy as jnp
from jax import lax

HEADS = 64
KV_HEADS = 8
HEAD_DIM = 128
PAGE = 256
STEPS = 3
CAP = 2
REQ_INST = 8
POOL = 128
RANGES = 16
INSTANCES = 16
REQUESTS = 128


def lend_map(key):
    full_home = jax.random.randint(jax.random.fold_in(key, 11), (), 0, INSTANCES)
    slot_total = INSTANCES * CAP
    range_ids = jnp.arange(RANGES, dtype=jnp.int32)

    def one_lender(lender_key, crowded):
        cut_key, tail_key, order_key, shuffle_key, owner_key = jax.random.split(lender_key, 5)
        cuts = jnp.sort(jax.random.permutation(cut_key, POOL - 1)[:RANGES - 1] + 1).astype(jnp.int32)
        bounds = jnp.concatenate([jnp.zeros((1,), jnp.int32), cuts, jnp.full((1,), POOL, jnp.int32)])
        packed = jnp.concatenate([jnp.zeros((1,), jnp.int32), POOL - RANGES + 1 + range_ids])
        bounds = jnp.where(crowded, packed, bounds)
        page_count = bounds[1:] - bounds[:-1]
        start = bounds[:-1]
        tail = jax.random.randint(tail_key, (RANGES,), 0, PAGE)
        tail = jnp.where(crowded & (range_ids == 0), 0, tail)
        tokens = page_count * PAGE - tail
        order = jax.random.permutation(order_key, slot_total).astype(jnp.int32)
        slot_ids = jnp.arange(slot_total, dtype=jnp.int32)
        slot_home = slot_ids // CAP
        ranking = jnp.where(slot_home == full_home, slot_ids - 3 * slot_total, order)
        ranking = jnp.where(slot_ids == 0, -2 * slot_total, ranking)
        ranking = jnp.where(slot_ids == slot_total - 1, -2 * slot_total + 1, ranking)
        chosen = jnp.argsort(ranking)[:RANGES]
        chosen = chosen[jax.random.permutation(shuffle_key, RANGES)]
        homes = slot_home[chosen]
        local = jax.random.randint(owner_key, (RANGES,), 0, REQ_INST)
        local = jnp.where(chosen == 0, 0, local)
        local = jnp.where(chosen == slot_total - 1, REQ_INST - 1, local)
        owner = homes * REQ_INST + local
        return (owner.astype(jnp.int32), start.astype(jnp.int32), tokens.astype(jnp.int32))
    lender_keys = jax.random.split(jax.random.fold_in(key, 12), INSTANCES)
    crowded_flags = jnp.arange(INSTANCES) == 0
    return jax.vmap(one_lender)(lender_keys, crowded_flags)


def draw_range_owner(key, part):
    return lend_map(key)[0]


def draw_range_start(key, part):
    return lend_map(key)[1]


def draw_range_tokens(key, part):
    return lend_map(key)[2]


def draw_page_cache(key, part):
    key = jax.random.fold_in(key, 3)
    first_key = jax.random.fold_in(key, 0)
    shape = (INSTANCES * POOL, 2, PAGE, KV_HEADS * HEAD_DIM)
    values = jnp.clip(jax.random.normal(first_key, shape, jnp.float32), -6.0, 6.0)
    return values.astype(jnp.bfloat16)


def draw_queries(key, part):
    key = jax.random.fold_in(key, 1)
    first_key, scale_key = jax.random.split(key)
    row_scale = jnp.exp(jax.random.uniform(scale_key, (STEPS, REQUESTS, HEADS, 1), jnp.float32, math.log(0.5), math.log(2.0)))
    values = jnp.clip(jax.random.normal(first_key, (STEPS, REQUESTS, HEADS, HEAD_DIM), jnp.float32), -4.0, 4.0) * row_scale
    return values.reshape(STEPS, REQUESTS, HEADS * HEAD_DIM).astype(jnp.bfloat16)


def draw_new_kv(key, part):
    key = jax.random.fold_in(key, 2)
    first_key, value_key = jax.random.split(key)
    value_rows = jnp.clip(jax.random.normal(value_key, (STEPS, REQUESTS, KV_HEADS, HEAD_DIM), jnp.float32), -4.0, 4.0)
    key_rows = jnp.clip(jax.random.normal(first_key, (STEPS, REQUESTS, KV_HEADS, HEAD_DIM), jnp.float32), -4.0, 4.0)
    return jnp.stack([key_rows, value_rows], axis=2).reshape(STEPS, REQUESTS, 2, KV_HEADS * HEAD_DIM).astype(jnp.bfloat16)


def setup_inputs(seed: int = 0) -> dict:
    streams_of = jax.random.split(jax.random.key(seed), 7)
    queries = draw_queries(jax.random.fold_in(streams_of[6], 71), 0)
    new_kv = draw_new_kv(jax.random.fold_in(streams_of[6], 71), 0)
    page_cache = draw_page_cache(jax.random.fold_in(streams_of[6], 71), 0)
    range_owner = draw_range_owner(jax.random.fold_in(streams_of[6], 71), 0)
    range_start = draw_range_start(jax.random.fold_in(streams_of[6], 71), 0)
    range_tokens = draw_range_tokens(jax.random.fold_in(streams_of[6], 71), 0)
    return dict(queries=queries, new_kv=new_kv, page_cache=page_cache, range_owner=range_owner, range_start=range_start, range_tokens=range_tokens)


VERY_LOW = -1e+30

def page_layout(owner, start, tokens):
    page_count = (tokens + PAGE - 1) // PAGE
    page_ids = jnp.arange(POOL, dtype=jnp.int32)
    page_hot = (page_ids[:, None] >= start[None, :]) & (page_ids[:, None] < (start + page_count)[None, :])
    page_owner = lax.optimization_barrier(jnp.sum(jnp.where(page_hot, owner[None, :], 0), axis=1)).astype(jnp.int32)
    page_first = lax.optimization_barrier(jnp.sum(jnp.where(page_hot, start[None, :], 0), axis=1)).astype(jnp.int32)
    page_limit = lax.optimization_barrier(jnp.sum(jnp.where(page_hot, tokens[None, :], 0), axis=1)).astype(jnp.int32)
    position = (page_ids - page_first)[:, None] * PAGE + jnp.arange(PAGE, dtype=jnp.int32)[None, :]
    usable = position < page_limit[:, None]
    return (page_owner, usable)

def reference(queries, new_kv, page_cache, range_owner, range_start, range_tokens):
    group_size = HEADS // KV_HEADS
    score_scale = 1.0 / math.sqrt(HEAD_DIM)
    query_rows = queries.astype(jnp.float32).reshape(STEPS, REQUESTS, KV_HEADS, group_size, HEAD_DIM)
    fresh_keys = new_kv[:, :, 0].astype(jnp.float32).reshape(STEPS, REQUESTS, KV_HEADS, HEAD_DIM)
    fresh_values = new_kv[:, :, 1].astype(jnp.float32).reshape(STEPS, REQUESTS, KV_HEADS, HEAD_DIM)
    fresh_scores = jnp.einsum('srkgd,trkd->srkgt', query_rows, fresh_keys) * score_scale
    causal = (jnp.arange(STEPS)[None, :] <= jnp.arange(STEPS)[:, None])[:, None, None, None, :]
    fresh_scores = jnp.where(causal, fresh_scores, VERY_LOW)
    pools = page_cache.reshape(INSTANCES, POOL, 2, PAGE, KV_HEADS, HEAD_DIM)

    def page_scores(pool_pages, owner, start, tokens):
        page_owner, usable = page_layout(owner, start, tokens)
        key_rows = pool_pages[:, 0].astype(jnp.float32)
        scores = jnp.einsum('spkgd,pikd->spkgi', query_rows[:, page_owner], key_rows) * score_scale
        return (jnp.where(usable[None, :, None, None, :], scores, VERY_LOW), page_owner, usable)

    def find_max(row_max, lender):
        scores, page_owner, usable = page_scores(*lender)
        return (row_max.at[:, page_owner].max(lax.optimization_barrier(jnp.max(scores, axis=4))), None)
    lenders = (pools, range_owner, range_start, range_tokens)
    row_max, _ = lax.scan(find_max, lax.optimization_barrier(jnp.max(fresh_scores, axis=4)), lenders)

    def accumulate(carry, lender):
        numerator, denominator = carry
        scores, page_owner, usable = page_scores(*lender)
        weights = jnp.where(usable[None, :, None, None, :], jnp.exp(scores - row_max[:, page_owner][..., None]), 0.0)
        rounded = lax.optimization_barrier(weights.astype(jnp.bfloat16)).astype(jnp.float32)
        value_rows = lender[0][:, 1].astype(jnp.float32)
        contribution = jnp.einsum('spkgi,pikd->spkgd', rounded, value_rows)
        numerator = numerator.at[:, page_owner].add(contribution)
        denominator = denominator.at[:, page_owner].add(lax.optimization_barrier(jnp.sum(weights, axis=4)))
        return ((numerator, denominator), None)
    start_numerator = jnp.zeros((STEPS, REQUESTS, KV_HEADS, group_size, HEAD_DIM), jnp.float32)
    start_denominator = jnp.zeros((STEPS, REQUESTS, KV_HEADS, group_size), jnp.float32)
    (numerator, denominator), _ = lax.scan(accumulate, (start_numerator, start_denominator), lenders)
    fresh_weights = jnp.where(causal, jnp.exp(fresh_scores - row_max[..., None]), 0.0)
    fresh_rounded = lax.optimization_barrier(fresh_weights.astype(jnp.bfloat16)).astype(jnp.float32)
    numerator = numerator + jnp.einsum('srkgt,trkd->srkgd', fresh_rounded, fresh_values)
    denominator = denominator + lax.optimization_barrier(jnp.sum(fresh_weights, axis=4))
    result = numerator / denominator[..., None]
    return result.reshape(STEPS, REQUESTS, HEADS * HEAD_DIM).astype(jnp.bfloat16)
```

```python
import functools
import math

import jax
import jax.numpy as jnp
from jax import lax
from jax.experimental import pallas as pl
from jax.experimental.pallas import tpu as pltpu
from jax.sharding import PartitionSpec as P

HEAD_DIM = 128
PAGE = 256
CAP = 2
REQ_INST = 8
CHUNK = 16
VERY_LOW = -1e30
FLOOR = -1e29

f32 = jnp.float32
bf16 = jnp.bfloat16


def attend(groups, slice_tokens, meta, q_ref, k_ref, v_ref, out_ref, slot, qf, of, mf, lf):
    sources, ranges = q_ref.shape[0], q_ref.shape[1]
    rows = sources * groups
    half = rows // 2
    pages = k_ref.shape[0]
    extra = (pages - ranges) // CHUNK
    chunk_tokens = CHUNK * slice_tokens
    scale = 1.0 / math.sqrt(HEAD_DIM)
    exp2_scale = scale * math.log2(math.e)
    my_tp = meta[2, 0]

    for e in range(extra):
        slot[0, e] = 0
        slot[1, e] = 0
        slot[2, e] = 0
        slot[3, e] = 0

    def fill(r, count):
        start = meta[0, r]
        tokens = meta[1, r]
        span = (tokens + PAGE - 1) // PAGE
        more = (span - 1) // CHUNK
        tail = jnp.clip(tokens % PAGE - my_tp * slice_tokens, 0, slice_tokens)
        high = start * slice_tokens + (tokens // PAGE) * slice_tokens + tail
        slot[4, r] = high

        def one(j, carry):
            first = start + (j + 1) * CHUNK
            slot[0, count + j] = jnp.minimum(first, pages - CHUNK)
            slot[1, count + j] = first * slice_tokens
            slot[2, count + j] = high
            slot[3, count + j] = r
            return carry

        lax.fori_loop(0, more, one, 0)
        return count + more

    lax.fori_loop(0, ranges, fill, 0)

    for x in range(sources):
        for g in range(groups):
            qf[pl.ds((x * groups + g) * ranges, ranges), :] = q_ref[
                x, :, g * HEAD_DIM : (g + 1) * HEAD_DIM
            ].astype(f32)

    row_id = lax.broadcasted_iota(jnp.int32, (rows, HEAD_DIM), 0)
    lane_id = lax.broadcasted_iota(jnp.int32, (rows, chunk_tokens), 1)
    top = row_id < half

    def chunk(r, page, low, high):
        q = qf[pl.ds(r, rows, stride=ranges), :]
        zero = jnp.zeros_like(q)
        wide = jnp.concatenate(
            [jnp.where(top, q, zero), jnp.where(top, zero, q)], axis=1
        ).astype(bf16)
        k = k_ref[pl.ds(page, CHUNK), 0].reshape(chunk_tokens, 2 * HEAD_DIM)
        v = v_ref[pl.ds(page, CHUNK), 0].reshape(chunk_tokens, 2 * HEAD_DIM)
        s = lax.dot_general(wide, k, (((1,), (1,)), ((), ())), preferred_element_type=f32)
        place = lane_id + page * slice_tokens
        s = jnp.where((place >= low) & (place < high), s, VERY_LOW)
        m = jnp.maximum(jnp.max(s, axis=1, keepdims=True), FLOOR)
        p = jnp.exp2((s - m) * exp2_scale)
        total = jnp.sum(p, axis=1, keepdims=True)
        o = jnp.dot(p.astype(bf16), v, preferred_element_type=f32)
        o = jnp.where(top, o[:, :HEAD_DIM], o[:, HEAD_DIM:])
        shape = (rows, HEAD_DIM)
        return o, jnp.broadcast_to(m, shape), jnp.broadcast_to(total, shape)

    for r in range(ranges):
        start = meta[0, r]
        o, m, total = chunk(
            r, jnp.minimum(start, pages - CHUNK), start * slice_tokens, slot[4, r]
        )
        of[pl.ds(r, rows, stride=ranges), :] = o
        mf[pl.ds(r, rows, stride=ranges), :] = m
        lf[pl.ds(r, rows, stride=ranges), :] = total

    more = [chunk(slot[3, e], slot[0, e], slot[1, e], slot[2, e]) for e in range(extra)]
    for e in range(extra):
        o, m, total = more[e]
        at = pl.ds(slot[3, e], rows, stride=ranges)
        m_old = mf[at, :]
        m_new = jnp.maximum(m_old, m)
        a_old = jnp.exp2((m_old - m_new) * exp2_scale)
        a = jnp.exp2((m - m_new) * exp2_scale)
        of[at, :] = of[at, :] * a_old + o * a
        lf[at, :] = lf[at, :] * a_old + total * a
        mf[at, :] = m_new

    lane = lax.broadcasted_iota(jnp.int32, (ranges, HEAD_DIM), 1)
    for x in range(sources):
        stats = jnp.zeros((ranges, HEAD_DIM), f32)
        for g in range(groups):
            at = pl.ds((x * groups + g) * ranges, ranges)
            total = lf[at, :]
            some = total > 0.0
            safe = jnp.where(some, total, 1.0)
            out_ref[x, :, g * HEAD_DIM : (g + 1) * HEAD_DIM] = (of[at, :] / safe).astype(bf16)
            lse = jnp.where(some, mf[at, :] * scale + jnp.log(safe), VERY_LOW)
            mine = (lane == g) | (lane == g + groups) | (lane == g + 2 * groups)
            stats = jnp.where(mine, lse, stats)
        out_ref[x, :, groups * HEAD_DIM :] = split3(stats, lane, groups)


def split3(stats, lane, groups):
    high = stats.astype(bf16).astype(f32)
    rest = stats - high
    mid = rest.astype(bf16).astype(f32)
    low = rest - mid
    return jnp.where(lane < groups, high, jnp.where(lane < 2 * groups, mid, low)).astype(bf16)


def join3(parts, groups):
    parts = parts.astype(f32)
    return (
        parts
        + pltpu.roll(parts, HEAD_DIM - groups, 1)
        + pltpu.roll(parts, HEAD_DIM - 2 * groups, 1)
    )


def merge_sources(groups, in_ref, pick_ref, out_ref):
    sources, ranges = in_ref.shape[0], in_ref.shape[1]
    lane = lax.broadcasted_iota(jnp.int32, (ranges, HEAD_DIM), 1)
    lses = [join3(in_ref[i, :, groups * HEAD_DIM :], groups) for i in range(sources)]
    top = functools.reduce(jnp.maximum, lses)
    shares = [jnp.exp(l - top) for l in lses]
    total = functools.reduce(jnp.add, shares)
    lse = top + jnp.log(total)
    inverse = 1.0 / total
    shares = [s * inverse for s in shares]
    pick = pick_ref[...]
    stats = jnp.zeros((ranges, HEAD_DIM), f32)
    for g in range(groups):
        cols = slice(g * HEAD_DIM, (g + 1) * HEAD_DIM)
        acc = jnp.zeros((ranges, HEAD_DIM), f32)
        for i in range(sources):
            acc = acc + shares[i][:, g : g + 1] * in_ref[i, :, cols].astype(f32)
        out_ref[:, cols] = jnp.dot(pick, acc.astype(bf16), preferred_element_type=f32).astype(bf16)
        mine = (lane == g) | (lane == g + groups) | (lane == g + 2 * groups)
        stats = jnp.where(mine, jnp.broadcast_to(lse[:, g : g + 1], stats.shape), stats)
    parts = split3(stats, lane, groups)
    out_ref[:, groups * HEAD_DIM :] = jnp.dot(pick, parts, preferred_element_type=f32).astype(bf16)


def finish(steps, heads, in_ref, owner_ref, q_ref, k_ref, v_ref, out_ref):
    groups = steps * heads
    requests = q_ref.shape[1]
    scale = 1.0 / math.sqrt(HEAD_DIM)
    stats = join3(in_ref[:, groups * HEAD_DIM :], groups)
    lses = jnp.transpose(stats, (1, 0))
    owned = owner_ref[...] == lax.broadcasted_iota(jnp.int32, owner_ref.shape, 0)
    keys = [k_ref[t].astype(f32) for t in range(steps)]
    values = [v_ref[t].astype(f32) for t in range(steps)]
    for s in range(steps):
        for h in range(heads):
            g = s * heads + h
            cols = slice(h * HEAD_DIM, (h + 1) * HEAD_DIM)
            q = q_ref[s, :, cols].astype(f32)
            scores = [
                jnp.sum(q * keys[t], axis=1, keepdims=True) * scale for t in range(s + 1)
            ]
            lent = jnp.where(owned, jnp.broadcast_to(lses[g : g + 1, :], owned.shape), VERY_LOW)
            top = functools.reduce(jnp.maximum, scores)
            top = jnp.maximum(top, jnp.max(lent, axis=1, keepdims=True))
            share = jnp.where(owned, jnp.exp(lent - top), 0.0)
            total = jnp.sum(share, axis=1, keepdims=True)
            acc = jnp.dot(
                share,
                in_ref[:, g * HEAD_DIM : (g + 1) * HEAD_DIM].astype(f32),
                preferred_element_type=f32,
                precision=lax.Precision.HIGHEST,
            )
            for t in range(s + 1):
                weight = jnp.exp(scores[t] - top)
                total = total + weight
                acc = acc + weight.astype(bf16).astype(f32) * values[t]
            out_ref[s, :, cols] = (acc / total).astype(bf16)


def slot_ranks(homes):
    count = homes.shape[1]
    earlier = jnp.arange(count)[None, :] < jnp.arange(count)[:, None]
    matches = homes[:, :, None] == homes[:, None, :]
    return jnp.sum(matches & earlier[None], axis=2)


def on_device(queries, new_kv, page_cache, range_owner, range_start, range_tokens):
    steps, requests, columns = queries.shape
    lenders = lax.axis_size("inst")
    tp_count = lax.axis_size("tp")
    my_inst = lax.axis_index("inst")
    my_tp = lax.axis_index("tp")
    pages, _, slice_tokens, kv_columns = page_cache.shape
    ranges = range_owner.shape[1]
    heads = columns // HEAD_DIM
    groups = steps * heads
    kv_heads = kv_columns // HEAD_DIM
    group_size = heads * tp_count // kv_heads
    slots = lenders * CAP
    wide = (groups + 1) * HEAD_DIM
    pairs = kv_heads // 2
    sources = tp_count // pairs

    homes = range_owner // REQ_INST
    ranks = slot_ranks(homes)
    hit = (homes == my_inst)[:, :, None] & (ranks[:, :, None] == jnp.arange(CAP))
    slot_owner = (
        jnp.sum(jnp.where(hit, (range_owner - my_inst * REQ_INST + 1)[:, :, None], 0), axis=1) - 1
    ).reshape(slots)
    my_slot = lax.dynamic_index_in_dim(homes * CAP + ranks, my_inst, 0, keepdims=False)
    slot_pick = (jnp.arange(slots)[:, None] == my_slot[None, :]).astype(bf16)
    owner_pick = (slot_owner[:, None] == jnp.arange(requests)[None, :]).astype(bf16)

    sent = jnp.einsum("lr,srx->lsx", owner_pick, queries, preferred_element_type=f32).astype(bf16)
    sent = sent.reshape(lenders, CAP, groups * HEAD_DIM)
    got = lax.all_to_all(sent, "inst", split_axis=0, concat_axis=0, tiled=True)
    mine = jnp.einsum(
        "lr,lx->rx", slot_pick, got.reshape(slots, -1), preferred_element_type=f32
    ).astype(bf16)
    every = lax.all_gather(mine, "tp", axis=0, tiled=False)

    meta = jnp.stack(
        [
            lax.dynamic_index_in_dim(range_start, my_inst, 0, keepdims=False),
            lax.dynamic_index_in_dim(range_tokens, my_inst, 0, keepdims=False),
            jnp.full((ranges,), my_tp, jnp.int32),
        ]
    )
    pair_columns = 2 * HEAD_DIM
    partial = pl.pallas_call(
        functools.partial(attend, groups, slice_tokens),
        grid=(pairs,),
        in_specs=[
            pl.BlockSpec(memory_space=pltpu.SMEM),
            pl.BlockSpec((sources, ranges, groups * HEAD_DIM), lambda i: (i, 0, 0)),
            pl.BlockSpec((pages, 1, slice_tokens, pair_columns), lambda i: (0, 0, 0, i)),
            pl.BlockSpec((pages, 1, slice_tokens, pair_columns), lambda i: (0, 1, 0, i)),
        ],
        out_specs=pl.BlockSpec((sources, ranges, wide), lambda i: (i, 0, 0)),
        out_shape=jax.ShapeDtypeStruct((tp_count, ranges, wide), bf16),
        scratch_shapes=[pltpu.SMEM((5, ranges), jnp.int32)]
        + [pltpu.VMEM((sources * groups * ranges, HEAD_DIM), f32)] * 4,
        compiler_params=pltpu.CompilerParams(vmem_limit_bytes=48 * 2**20),
        name="attend",
    )(meta, every, page_cache, page_cache)

    parts = lax.all_to_all(partial, "tp", split_axis=0, concat_axis=0, tiled=True)
    vmem = pl.BlockSpec(memory_space=pltpu.VMEM)
    lent = pl.pallas_call(
        functools.partial(merge_sources, groups),
        in_specs=[vmem] * 2,
        out_specs=vmem,
        out_shape=jax.ShapeDtypeStruct((slots, wide), bf16),
        compiler_params=pltpu.CompilerParams(vmem_limit_bytes=32 * 2**20),
        name="merge_sources",
    )(parts, slot_pick)
    back = lax.all_to_all(
        lent.reshape(lenders, CAP, wide), "inst", split_axis=0, concat_axis=0, tiled=True
    ).reshape(slots, wide)

    head = my_tp * heads // group_size
    fresh = lax.dynamic_slice_in_dim(new_kv, head * HEAD_DIM, HEAD_DIM, axis=3)
    owner_rows = jnp.broadcast_to(slot_owner[None, :], (requests, slots))
    return pl.pallas_call(
        functools.partial(finish, steps, heads),
        in_specs=[vmem] * 5,
        out_specs=vmem,
        out_shape=jax.ShapeDtypeStruct((steps, requests, columns), bf16),
        compiler_params=pltpu.CompilerParams(vmem_limit_bytes=32 * 2**20),
        name="finish",
    )(back, owner_rows, queries, fresh[:, :, 0], fresh[:, :, 1])


def solution(mesh):
    placed = (
        P(None, "inst", "tp"),
        P(None, "inst", None, None),
        P("inst", None, "tp", None),
        P(),
        P(),
        P(),
    )
    return jax.shard_map(
        on_device, mesh=mesh, in_specs=placed, out_specs=P(None, "inst", "tp"), check_vma=False
    )
```

```python
import functools
import math

import jax
import jax.numpy as jnp
from jax import lax
from jax.experimental import pallas as pl
from jax.experimental.pallas import tpu as pltpu
from jax.sharding import PartitionSpec as P

HEAD_DIM = 128
PAGE = 256
CAP = 2
REQ_INST = 8
SIDE = 4
SHIFTS = (1, 3, 2)
CHUNK = 16
BATCH = 8
MORE = 4
VERY_LOW = -1e30
FLOOR = -1e29
PAD = 16
PAGE_ROW, LOW_ROW, HIGH_ROW, RANGE_ROW, END_ROW, PLACE_ROW, START_ROW, SLOT_ROW = range(8)

f32 = jnp.float32
bf16 = jnp.bfloat16


def iota(shape, dim):
    return lax.broadcasted_iota(jnp.int32, shape, dim)


def split3(stats, lane, groups):
    high = stats.astype(bf16).astype(f32)
    rest = stats - high
    mid = rest.astype(bf16).astype(f32)
    low = rest - mid
    return jnp.where(lane < groups, high, jnp.where(lane < 2 * groups, mid, low)).astype(bf16)


def join3(parts, groups):
    parts = parts.astype(f32)
    return (
        parts
        + pltpu.roll(parts, HEAD_DIM - groups, 1)
        + pltpu.roll(parts, HEAD_DIM - 2 * groups, 1)
    )


def prepare(q_ref, owner_ref, sent_ref, mine_ref, stage):
    steps, requests, columns = q_ref.shape
    heads = columns // HEAD_DIM
    groups = steps * heads
    lenders, ranges = owner_ref.shape
    owner = owner_ref[...]
    hit = owner // REQ_INST == lax.axis_index("inst")
    earlier = (iota((ranges, ranges), 0) < iota((ranges, ranges), 1)).astype(f32)
    rank = jnp.dot(hit.astype(f32), earlier, preferred_element_type=f32)
    local = (owner % REQ_INST + 1).astype(f32)
    owners = []
    for c in range(CAP):
        chosen = jnp.where(hit & (jnp.abs(rank - c) < 0.5), local, 0.0)
        mine = jnp.sum(chosen, axis=1, keepdims=True) - 1.0
        owners.append(jnp.broadcast_to(mine, (lenders, HEAD_DIM)))
        pick = (mine.astype(jnp.int32) == iota((lenders, requests), 1)).astype(f32)
        for s in range(steps):
            value = jnp.dot(pick, q_ref[s].astype(f32), preferred_element_type=f32)
            for h in range(heads):
                at = pl.ds(c * groups + s * heads + h, lenders, stride=CAP * groups)
                stage[at, :] = value[:, h * HEAD_DIM : (h + 1) * HEAD_DIM]
    sent_ref[...] = stage[...].astype(bf16)
    mine_ref[...] = jnp.transpose(jnp.concatenate(owners, axis=0), (1, 0))[: mine_ref.shape[0], :]


def make_plan(slice_tokens, pages, owner_ref, start_ref, tokens_ref, plan):
    ranges = owner_ref.shape[1]
    me = lax.axis_index("inst")
    my_tp = lax.axis_index("tp")
    for i in range(plan.shape[0]):
        for r in range(ranges):
            plan[i, r] = 0
    plan[PLACE_ROW, 1] = my_tp % SIDE
    plan[PLACE_ROW, 2] = my_tp // SIDE

    def fill(r, count):
        start = start_ref[me, r]
        tokens = tokens_ref[me, r]
        span = (tokens + PAGE - 1) // PAGE
        more = (span - 1) // CHUNK
        tail = jnp.clip(tokens % PAGE - my_tp * slice_tokens, 0, slice_tokens)
        high = (start + tokens // PAGE) * slice_tokens + tail
        plan[END_ROW, r] = high
        plan[START_ROW, r] = start

        def one(j, carry):
            first = start + (j + 1) * CHUNK
            plan[PAGE_ROW, count + j] = jnp.minimum(first, pages - CHUNK)
            plan[LOW_ROW, count + j] = first * slice_tokens
            plan[HIGH_ROW, count + j] = high
            plan[RANGE_ROW, count + j] = r
            return carry

        lax.fori_loop(0, more, one, 0)
        return count + more

    plan[PLACE_ROW, 0] = lax.fori_loop(0, ranges, fill, 0)
    homes = [owner_ref[me, r] // REQ_INST for r in range(ranges)]
    for r in range(ranges):
        rank = sum([(homes[e] == homes[r]).astype(jnp.int32) for e in range(r)], jnp.int32(0))
        plan[SLOT_ROW, r] = homes[r] * CAP + rank


def slot_matrix(plan, shape, range_dim):
    ranges = shape[range_dim]
    matrix = jnp.zeros(shape, f32)
    for r in range(ranges):
        here = (iota(shape, range_dim) == r) & (iota(shape, 1 - range_dim) == plan[SLOT_ROW, r])
        matrix = jnp.where(here, 1.0, matrix)
    return matrix


def pick_ranges(groups, plan, got_ref, out_ref, stage):
    ranges = out_ref.shape[0]
    slots = got_ref.shape[0] // groups
    stage[...] = got_ref[...].astype(f32)
    matrix = slot_matrix(plan, (ranges, slots), 0)
    for g in range(groups):
        value = stage[pl.ds(g, slots, stride=groups), :]
        out_ref[:, g * HEAD_DIM : (g + 1) * HEAD_DIM] = jnp.dot(
            matrix, value, preferred_element_type=f32
        ).astype(bf16)


def attend_row(groups, ranges, plan, chunks, k_ref, v_ref, out_ref, qf, of, mf, lf):
    rows = SIDE * groups
    half = rows // 2
    pages, _, slice_tokens, _ = k_ref.shape
    chunk_tokens = CHUNK * slice_tokens
    scale = 1.0 / math.sqrt(HEAD_DIM)
    exp2_scale = scale * math.log2(math.e)
    place = plan[PLACE_ROW, 1]
    sources = [(place + SIDE - k) % SIDE for k in (0,) + SHIFTS]

    for x, chunk in zip(sources, chunks):
        base = pl.multiple_of(x * (groups * ranges), groups * ranges)
        for g in range(groups):
            qf[pl.ds(base + g * ranges, ranges), :] = chunk[
                :, g * HEAD_DIM : (g + 1) * HEAD_DIM
            ].astype(f32)

    top = iota((rows, HEAD_DIM), 0) < half
    lane = iota((1, chunk_tokens), 1)

    def load(ref, page):
        return ref[pl.ds(page, CHUNK), 0].reshape(chunk_tokens, 2 * HEAD_DIM)

    def scores(r, page, low, high):
        q = qf[pl.ds(r, rows, stride=ranges), :]
        zero = jnp.zeros_like(q)
        wide = jnp.concatenate(
            [jnp.where(top, q, zero), jnp.where(top, zero, q)], axis=1
        ).astype(bf16)
        s = lax.dot_general(
            wide, load(k_ref, page), (((1,), (1,)), ((), ())), preferred_element_type=f32
        )
        at = lane + page * slice_tokens
        return s + jnp.where((at >= low) & (at < high), 0.0, VERY_LOW)

    def softmax(s):
        m = jnp.maximum(jnp.max(s, axis=1, keepdims=True), FLOOR)
        p = jnp.exp2((s - m) * exp2_scale)
        return p, m, jnp.sum(p, axis=1, keepdims=True)

    def values(p, page):
        o = jnp.dot(p.astype(bf16), load(v_ref, page), preferred_element_type=f32)
        return jnp.where(top, o[:, :HEAD_DIM], o[:, HEAD_DIM:])

    def many(work):
        s = [scores(*w) for w in work]
        s = [softmax(one) for one in s]
        o = [values(one[0], w[1]) for one, w in zip(s, work)]
        return [(one, m, total) for one, (_, m, total) in zip(o, s)]

    def first(b, carry):
        work = []
        for j in range(BATCH):
            r = b * BATCH + j
            start = plan[START_ROW, r]
            page = jnp.minimum(start, pages - CHUNK)
            work.append((r, page, start * slice_tokens, plan[END_ROW, r]))
        for w, (o, m, total) in zip(work, many(work)):
            at = pl.ds(w[0], rows, stride=ranges)
            of[at, :] = o
            mf[at, :] = jnp.broadcast_to(m, o.shape)
            lf[at, :] = jnp.broadcast_to(total, o.shape)
        return carry

    lax.fori_loop(0, ranges // BATCH, first, 0)

    def more(b, carry):
        work = []
        for j in range(MORE):
            e = b * MORE + j
            work.append((plan[RANGE_ROW, e], plan[PAGE_ROW, e], plan[LOW_ROW, e], plan[HIGH_ROW, e]))
        for w, (o, m, total) in zip(work, many(work)):
            at = pl.ds(w[0], rows, stride=ranges)
            m_old = mf[at, :]
            m_new = jnp.maximum(m_old, m)
            a_old = jnp.exp2((m_old - m_new) * exp2_scale)
            a = jnp.exp2((m - m_new) * exp2_scale)
            of[at, :] = of[at, :] * a_old + o * a
            lf[at, :] = lf[at, :] * a_old + total * a
            mf[at, :] = m_new
        return carry

    lax.fori_loop(0, (plan[PLACE_ROW, 0] + MORE - 1) // MORE, more, 0)

    lanes = iota((ranges, HEAD_DIM), 1)
    for x in range(SIDE):
        m = jnp.zeros((ranges, HEAD_DIM), f32)
        totals = jnp.zeros((ranges, HEAD_DIM), f32)
        for g in range(groups):
            at = pl.ds((x * groups + g) * ranges, ranges)
            total = lf[at, :]
            safe = jnp.where(total > 0.0, total, 1.0)
            out_ref[x, :, g * HEAD_DIM : (g + 1) * HEAD_DIM] = (of[at, :] / safe).astype(bf16)
            mine = (lanes == g) | (lanes == g + groups) | (lanes == g + 2 * groups)
            m = jnp.where(mine, mf[at, :], m)
            totals = jnp.where(mine, total, totals)
        some = totals > 0.0
        lse = jnp.where(some, m * scale + jnp.log(jnp.where(some, totals, 1.0)), VERY_LOW)
        out_ref[x, :, groups * HEAD_DIM :] = split3(lse, lanes, groups)


def attend_own(groups, plan, c0, c1, c2, c3, k_ref, v_ref, out_ref, *scratch):
    attend_row(groups, c0.shape[0], plan, [c0, c1, c2, c3], k_ref, v_ref, out_ref, *scratch)


def attend_others(groups, plan, b0, b1, b2, k_ref, v_ref, held, out_ref, q, *scratch):
    for i, block in enumerate((b0, b1, b2)):

        @pl.when(pl.program_id(0) == i)
        def _():
            q[...] = block[...]

    chunks = [q.at[j] for j in range(SIDE)]
    attend_row(groups, q.shape[1], plan, chunks, k_ref, v_ref, out_ref, *scratch)


def merge_sources(groups, plan, in_ref, out_ref, stage):
    sources, ranges = in_ref.shape[0], in_ref.shape[1]
    slots = out_ref.shape[0] // PAD
    lane = iota((ranges, HEAD_DIM), 1)
    lses = [join3(in_ref[i, :, groups * HEAD_DIM :], groups) for i in range(sources)]
    top = functools.reduce(jnp.maximum, lses)
    shares = [jnp.exp(l - top) for l in lses]
    total = functools.reduce(jnp.add, shares)
    lse = top + jnp.log(total)
    inverse = 1.0 / total
    shares = [s * inverse for s in shares]
    matrix = slot_matrix(plan, (slots, ranges), 1).astype(bf16)
    stats = jnp.zeros((ranges, HEAD_DIM), f32)
    for g in range(groups):
        cols = slice(g * HEAD_DIM, (g + 1) * HEAD_DIM)
        acc = jnp.zeros((ranges, HEAD_DIM), f32)
        for i in range(sources):
            acc = acc + shares[i][:, g : g + 1] * in_ref[i, :, cols].astype(f32)
        stage[pl.ds(g, slots, stride=PAD), :] = jnp.dot(
            matrix, acc.astype(bf16), preferred_element_type=f32
        )
        mine = (lane == g) | (lane == g + groups) | (lane == g + 2 * groups)
        stats = jnp.where(mine, jnp.broadcast_to(lse[:, g : g + 1], stats.shape), stats)
    parts = split3(stats, lane, groups)
    stage[pl.ds(groups, slots, stride=PAD), :] = jnp.dot(matrix, parts, preferred_element_type=f32)
    for g in range(groups + 1, PAD):
        stage[pl.ds(g, slots, stride=PAD), :] = jnp.zeros((slots, HEAD_DIM), f32)
    out_ref[...] = stage[...].astype(bf16)


def finish(steps, heads, in_ref, owner_ref, q_ref, k_ref, v_ref, out_ref, stage):
    groups = steps * heads
    lenders = in_ref.shape[0] // (CAP * PAD)
    scale = 1.0 / math.sqrt(HEAD_DIM)
    stage[...] = in_ref[...].astype(f32)

    def group(g):
        return jnp.concatenate(
            [stage[pl.ds(c * PAD + g, lenders, stride=CAP * PAD), :] for c in range(CAP)], axis=0
        )

    lses = jnp.transpose(join3(group(groups), groups), (1, 0))
    owned = owner_ref[...].astype(jnp.int32) == iota(owner_ref.shape, 0)
    keys = [k_ref[t].astype(f32) for t in range(steps)]
    values = [v_ref[t].astype(f32) for t in range(steps)]
    for s in range(steps):
        for h in range(heads):
            g = s * heads + h
            cols = slice(h * HEAD_DIM, (h + 1) * HEAD_DIM)
            q = q_ref[s, :, cols].astype(f32)
            scores = [
                jnp.sum(q * keys[t], axis=1, keepdims=True) * scale for t in range(s + 1)
            ]
            lent = jnp.where(owned, jnp.broadcast_to(lses[g : g + 1, :], owned.shape), VERY_LOW)
            top = functools.reduce(jnp.maximum, scores)
            top = jnp.maximum(top, jnp.max(lent, axis=1, keepdims=True))
            share = jnp.where(owned, jnp.exp(lent - top), 0.0)
            total = jnp.sum(share, axis=1, keepdims=True)
            acc = jnp.dot(
                share, group(g), preferred_element_type=f32, precision=lax.Precision.HIGHEST
            )
            for t in range(s + 1):
                weight = jnp.exp(scores[t] - top)
                total = total + weight
                acc = acc + weight.astype(bf16).astype(f32) * values[t]
            out_ref[s, :, cols] = (acc / total).astype(bf16)


def x_shift(k):
    return [(SIDE * y + x, SIDE * y + (x + k) % SIDE) for y in range(SIDE) for x in range(SIDE)]


def y_shift(k):
    return [(SIDE * y + x, SIDE * ((y + k) % SIDE) + x) for y in range(SIDE) for x in range(SIDE)]


def on_device(queries, new_kv, page_cache, range_owner, range_start, range_tokens):
    steps, requests, columns = queries.shape
    lenders = lax.axis_size("inst")
    tp_count = lax.axis_size("tp")
    my_tp = lax.axis_index("tp")
    pages, _, slice_tokens, kv_columns = page_cache.shape
    ranges = range_owner.shape[1]
    heads = columns // HEAD_DIM
    groups = steps * heads
    kv_heads = kv_columns // HEAD_DIM
    group_size = heads * tp_count // kv_heads
    slots = lenders * CAP
    wide = (groups + 1) * HEAD_DIM
    vmem = pl.BlockSpec(memory_space=pltpu.VMEM)
    smem = pl.BlockSpec(memory_space=pltpu.SMEM)
    small = pltpu.CompilerParams(vmem_limit_bytes=16 * 2**20)
    large = pltpu.CompilerParams(vmem_limit_bytes=32 * 2**20)

    sent, slot_owner = pl.pallas_call(
        prepare,
        in_specs=[vmem] * 2,
        out_specs=[vmem] * 2,
        out_shape=[
            jax.ShapeDtypeStruct((slots * groups, HEAD_DIM), bf16),
            jax.ShapeDtypeStruct((requests, slots), f32),
        ],
        scratch_shapes=[pltpu.VMEM((slots * groups, HEAD_DIM), f32)],
        compiler_params=small,
        name="prepare",
    )(queries, range_owner)
    got = lax.all_to_all(sent, "inst", split_axis=0, concat_axis=0, tiled=True)

    plan = pl.pallas_call(
        functools.partial(make_plan, slice_tokens, pages),
        in_specs=[smem] * 3,
        out_specs=smem,
        out_shape=jax.ShapeDtypeStruct((8, ranges), jnp.int32),
        name="make_plan",
    )(range_owner, range_start, range_tokens)
    head = my_tp * heads // group_size
    fresh = lax.dynamic_slice_in_dim(new_kv, head * HEAD_DIM, HEAD_DIM, axis=3)

    own = pl.pallas_call(
        functools.partial(pick_ranges, groups),
        in_specs=[smem, vmem],
        out_specs=vmem,
        out_shape=jax.ShapeDtypeStruct((ranges, groups * HEAD_DIM), bf16),
        scratch_shapes=[pltpu.VMEM((slots * groups, HEAD_DIM), f32)],
        compiler_params=small,
        name="pick_ranges",
    )(plan, got)
    chunks = [own] + [lax.ppermute(own, "tp", x_shift(k)) for k in SHIFTS]
    block = jnp.stack(chunks)
    blocks = [lax.ppermute(block, "tp", y_shift(k)) for k in SHIFTS]

    pair = 2 * HEAD_DIM
    scratch = [pltpu.VMEM((SIDE * groups * ranges, HEAD_DIM), f32)] * 4
    cost = dict(transcendentals=0)
    chunk_spec = pl.BlockSpec((ranges, groups * HEAD_DIM), lambda i, p: (0, 0))
    partial = pl.pallas_call(
        functools.partial(attend_own, groups),
        grid_spec=pltpu.PrefetchScalarGridSpec(
            num_scalar_prefetch=1,
            grid=(1,),
            in_specs=[chunk_spec] * SIDE
            + [
                pl.BlockSpec(
                    (pages, 1, slice_tokens, pair), lambda i, p, w=w: (0, w, 0, p[PLACE_ROW, 2])
                )
                for w in range(2)
            ],
            out_specs=pl.BlockSpec((SIDE, ranges, wide), lambda i, p: (p[PLACE_ROW, 2], 0, 0)),
            scratch_shapes=scratch,
        ),
        out_shape=jax.ShapeDtypeStruct((tp_count, ranges, wide), bf16),
        compiler_params=large,
        cost_estimate=pl.CostEstimate(flops=10**9, bytes_accessed=2**23, **cost),
        name="attend_own",
    )(plan, *chunks, page_cache, page_cache)

    def row_of(i, p):
        shift = jnp.where(i == 0, SHIFTS[0], jnp.where(i == 1, SHIFTS[1], SHIFTS[2]))
        return (p[PLACE_ROW, 2] + SIDE - shift) % SIDE

    block_spec = pl.BlockSpec((SIDE, ranges, groups * HEAD_DIM), lambda i, p: (0, 0, 0))
    partial = pl.pallas_call(
        functools.partial(attend_others, groups),
        grid_spec=pltpu.PrefetchScalarGridSpec(
            num_scalar_prefetch=1,
            grid=(len(SHIFTS),),
            in_specs=[block_spec] * len(SHIFTS)
            + [
                pl.BlockSpec(
                    (pages, 1, slice_tokens, pair), lambda i, p, w=w: (0, w, 0, row_of(i, p))
                )
                for w in range(2)
            ]
            + [pl.BlockSpec(memory_space=pl.ANY)],
            out_specs=pl.BlockSpec((SIDE, ranges, wide), lambda i, p: (row_of(i, p), 0, 0)),
            scratch_shapes=[pltpu.VMEM((SIDE, ranges, groups * HEAD_DIM), bf16)] + scratch,
        ),
        out_shape=jax.ShapeDtypeStruct((tp_count, ranges, wide), bf16),
        input_output_aliases={6: 0},
        compiler_params=large,
        cost_estimate=pl.CostEstimate(flops=3 * 10**9, bytes_accessed=3 * 2**23, **cost),
        name="attend_others",
    )(plan, *blocks, page_cache, page_cache, partial)

    parts = lax.all_to_all(partial, "tp", split_axis=0, concat_axis=0, tiled=True)
    lent = pl.pallas_call(
        functools.partial(merge_sources, groups),
        in_specs=[smem, vmem],
        out_specs=vmem,
        out_shape=jax.ShapeDtypeStruct((slots * PAD, HEAD_DIM), bf16),
        scratch_shapes=[pltpu.VMEM((slots * PAD, HEAD_DIM), f32)],
        compiler_params=small,
        name="merge_sources",
    )(plan, parts)
    back = lax.all_to_all(lent, "inst", split_axis=0, concat_axis=0, tiled=True)
    return pl.pallas_call(
        functools.partial(finish, steps, heads),
        in_specs=[vmem] * 5,
        out_specs=vmem,
        out_shape=jax.ShapeDtypeStruct((steps, requests, columns), bf16),
        scratch_shapes=[pltpu.VMEM((slots * PAD, HEAD_DIM), f32)],
        compiler_params=small,
        name="finish",
    )(back, slot_owner, queries, fresh[:, :, 0], fresh[:, :, 1])


def solution(mesh):
    placed = (
        P(None, "inst", "tp"),
        P(None, "inst", None, None),
        P("inst", None, "tp", None),
        P(),
        P(),
        P(),
    )
    return jax.shard_map(
        on_device, mesh=mesh, in_specs=placed, out_specs=P(None, "inst", "tp"), check_vma=False
    )
```

```python
import functools
import math

import jax
import jax.numpy as jnp
from jax import lax
from jax.experimental import pallas as pl
from jax.experimental.pallas import tpu as pltpu
from jax.sharding import PartitionSpec as P

HEAD_DIM = 128
PAGE = 256
CAP = 2
REQ_INST = 8
SIDE = 4
SHIFTS = (1, 3, 2)
FIRST = 8
CHUNK = 16
MORE = 8
VERY_LOW = -1e30
FLOOR = -1e29
PAD = 16
PAGE_ROW, LOW_ROW, HIGH_ROW, RANGE_ROW, END_ROW, COUNT_ROW, START_ROW = range(7)

f32 = jnp.float32
bf16 = jnp.bfloat16


def iota(shape, dim):
    return lax.broadcasted_iota(jnp.int32, shape, dim)


def split3(stats, lane, groups):
    high = stats.astype(bf16).astype(f32)
    rest = stats - high
    mid = rest.astype(bf16).astype(f32)
    low = rest - mid
    return jnp.where(lane < groups, high, jnp.where(lane < 2 * groups, mid, low)).astype(bf16)


def join3(parts, groups):
    parts = parts.astype(f32)
    return (
        parts
        + pltpu.roll(parts, HEAD_DIM - groups, 1)
        + pltpu.roll(parts, HEAD_DIM - 2 * groups, 1)
    )


def prepare(q_hbm, owner_hbm, sent_ref, mine_ref, q_ref, owner_ref, stage, sems):
    copies = [
        pltpu.make_async_copy(owner_hbm, owner_ref, sems.at[0]),
        pltpu.make_async_copy(q_hbm, q_ref, sems.at[1]),
    ]
    for copy in copies:
        copy.start()
    steps, requests, columns = q_ref.shape
    heads = columns // HEAD_DIM
    groups = steps * heads
    lenders, ranges = owner_ref.shape
    earlier = (iota((ranges, ranges), 0) < iota((ranges, ranges), 1)).astype(f32)
    copies[0].wait()
    owner = owner_ref[...]
    hit = owner // REQ_INST == lax.axis_index("inst")
    rank = jnp.dot(hit.astype(f32), earlier, preferred_element_type=f32)
    local = (owner % REQ_INST + 1).astype(f32)
    owners = []
    for c in range(CAP):
        chosen = jnp.where(hit & (jnp.abs(rank - c) < 0.5), local, 0.0)
        owners.append(jnp.sum(chosen, axis=1, keepdims=True) - 1.0)
    copies[1].wait()
    for c in range(CAP):
        pick = (owners[c].astype(jnp.int32) == iota((lenders, requests), 1)).astype(f32)
        for s in range(steps):
            value = jnp.dot(pick, q_ref[s].astype(f32), preferred_element_type=f32)
            for h in range(heads):
                at = pl.ds(c * groups + s * heads + h, lenders, stride=CAP * groups)
                stage[at, :] = value[:, h * HEAD_DIM : (h + 1) * HEAD_DIM]
    sent_ref[...] = stage[...].astype(bf16)
    spread = [jnp.broadcast_to(mine, (lenders, HEAD_DIM)) for mine in owners]
    mine_ref[...] = jnp.transpose(jnp.concatenate(spread, axis=0), (1, 0))[: mine_ref.shape[0], :]


def make_plan(slice_tokens, pages, owner_ref, start_ref, tokens_ref, plan, pick_ref, put_ref):
    ranges = owner_ref.shape[1]
    me = lax.axis_index("inst")
    my_tp = lax.axis_index("tp")
    for i in range(RANGE_ROW + 1):
        for r in range(ranges):
            plan[i, r] = 0

    def fill(r, count):
        start = start_ref[me, r]
        tokens = tokens_ref[me, r]
        span = (tokens + PAGE - 1) // PAGE
        more = jnp.maximum(span - FIRST + CHUNK - 1, 0) // CHUNK
        tail = jnp.clip(tokens % PAGE - my_tp * slice_tokens, 0, slice_tokens)
        high = (start + tokens // PAGE) * slice_tokens + tail
        plan[END_ROW, r] = high
        plan[START_ROW, r] = start

        def one(j, carry):
            first = start + FIRST + j * CHUNK
            plan[PAGE_ROW, count + j] = jnp.minimum(first, pages - CHUNK)
            plan[LOW_ROW, count + j] = first * slice_tokens
            plan[HIGH_ROW, count + j] = high
            plan[RANGE_ROW, count + j] = r
            return carry

        lax.fori_loop(0, more, one, 0)
        return count + more

    plan[COUNT_ROW, 0] = lax.fori_loop(0, ranges, fill, 0)
    homes = [owner_ref[me, r] // REQ_INST for r in range(ranges)]
    pick = jnp.zeros(pick_ref.shape, f32)
    put = jnp.zeros(put_ref.shape, f32)
    for r in range(ranges):
        rank = sum([(homes[e] == homes[r]).astype(jnp.int32) for e in range(r)], jnp.int32(0))
        slot = homes[r] * CAP + rank
        pick = jnp.where((iota(pick.shape, 0) == r) & (iota(pick.shape, 1) == slot), 1.0, pick)
        put = jnp.where((iota(put.shape, 1) == r) & (iota(put.shape, 0) == slot), 1.0, put)
    pick_ref[...] = pick
    put_ref[...] = put


def pick_ranges(groups, pick_ref, got_ref, out_ref, stage):
    slots = got_ref.shape[0] // groups
    stage[...] = got_ref[...].astype(f32)
    pick = pick_ref[...]
    for g in range(groups):
        value = stage[pl.ds(g, slots, stride=groups), :]
        out_ref[:, g * HEAD_DIM : (g + 1) * HEAD_DIM] = jnp.dot(
            pick, value, preferred_element_type=f32
        ).astype(bf16)


def place_before(shift):
    return (lax.axis_index("tp") // SIDE + SIDE - shift) % SIDE


def spread_queries(groups, chunks, qf, base):
    ranges = chunks[0].shape[0]
    for k, chunk in zip((0,) + SHIFTS, chunks):
        x = (lax.axis_index("tp") + SIDE - k) % SIDE
        at = pl.multiple_of(x * (groups * ranges) + base, groups * ranges)
        for g in range(groups):
            cols = slice(g * HEAD_DIM, (g + 1) * HEAD_DIM)
            qf[pl.ds(at + g * ranges, ranges), :] = chunk[:, cols].astype(f32)


def attend_row(groups, ranges, plan, k_ref, v_ref, wait_k, wait_v, out_ref, qf, base, of, lf):
    rows = SIDE * groups
    half = rows // 2
    pages, slice_tokens, pair = k_ref.shape
    scale = 1.0 / math.sqrt(HEAD_DIM)
    exp2_scale = scale * math.log2(math.e)
    top = iota((rows, HEAD_DIM), 0) < half

    def load(ref, page, span):
        return ref[pl.ds(page, span)].reshape(span * slice_tokens, pair)

    def scores(span, r, page, low, high):
        q = qf[pl.ds(base + r, rows, stride=ranges), :]
        zero = jnp.zeros_like(q)
        wide = jnp.concatenate(
            [jnp.where(top, q, zero), jnp.where(top, zero, q)], axis=1
        ).astype(bf16)
        k = load(k_ref, page, span)
        s = lax.dot_general(wide, k, (((1,), (1,)), ((), ())), preferred_element_type=f32)
        at = iota((1, span * slice_tokens), 1) + page * slice_tokens
        return s + jnp.where((at >= low) & (at < high), 0.0, VERY_LOW)

    def softmax(s):
        m = jnp.maximum(jnp.max(s, axis=1, keepdims=True), FLOOR)
        p = jnp.exp2((s - m) * exp2_scale)
        total = jnp.sum(p, axis=1, keepdims=True)
        some = total > 0.0
        safe = jnp.where(some, total, 1.0)
        lse = jnp.where(some, m * scale + jnp.log(safe), VERY_LOW)
        return p.astype(bf16), 1.0 / safe, jnp.broadcast_to(lse, (rows, HEAD_DIM))

    def values(span, page, p, inverse):
        o = jnp.dot(p, load(v_ref, page, span), preferred_element_type=f32)
        return jnp.where(top, o[:, :HEAD_DIM], o[:, HEAD_DIM:]) * inverse

    def many(span, work, wait=None):
        s = [scores(span, *w) for w in work]
        s = [softmax(one) for one in s]
        if wait is not None:
            wait()
        o = [values(span, w[1], one[0], one[1]) for one, w in zip(s, work)]
        return [(one, lse) for one, (_, _, lse) in zip(o, s)]

    def place(r):
        return pl.ds(pl.multiple_of(r * rows, 8), rows)

    work = []
    for r in range(ranges):
        start = plan[START_ROW, r]
        page = jnp.minimum(start, pages - FIRST)
        work.append((r, page, start * slice_tokens, plan[END_ROW, r]))
    wait_k()
    for w, (o, lse) in zip(work, many(FIRST, work, wait_v)):
        of[place(w[0]), :] = o
        lf[place(w[0]), :] = lse

    def more(b, carry):
        work = []
        for j in range(MORE):
            e = b * MORE + j
            work.append((plan[RANGE_ROW, e], plan[PAGE_ROW, e], plan[LOW_ROW, e], plan[HIGH_ROW, e]))
        for w, (o, lse) in zip(work, many(CHUNK, work)):
            at = place(w[0])
            old = lf[at, :]
            high = jnp.maximum(old, lse)
            share_old = jnp.exp(old - high)
            share = jnp.exp(lse - high)
            total = share_old + share
            of[at, :] = (of[at, :] * share_old + o * share) / total
            lf[at, :] = high + jnp.log(total)
        return carry

    lax.fori_loop(0, (plan[COUNT_ROW, 0] + MORE - 1) // MORE, more, 0)

    lanes = iota((ranges, HEAD_DIM), 1)
    for x in range(SIDE):
        lse = jnp.zeros((ranges, HEAD_DIM), f32)
        for g in range(groups):
            at = pl.ds(x * groups + g, ranges, stride=rows)
            out_ref[x, :, g * HEAD_DIM : (g + 1) * HEAD_DIM] = of[at, :].astype(bf16)
            mine = (lanes == g) | (lanes == g + groups) | (lanes == g + 2 * groups)
            lse = jnp.where(mine, lf[at, :], lse)
        out_ref[x, :, groups * HEAD_DIM :] = split3(lse, lanes, groups)


def cache_copies(cache, target, shift, sems, first):
    pair = target.shape[-1]
    y = place_before(shift)
    columns = pl.ds(pl.multiple_of(y * pair, pair), pair)
    return [
        pltpu.make_async_copy(cache.at[:, w, :, columns], target.at[w], sems.at[first + w])
        for w in range(2)
    ]


def row_copy(row, held, shift, sem):
    y = place_before(shift)
    return pltpu.make_async_copy(row, held.at[pl.ds(y * SIDE, SIDE)], sem)


def attend_own(groups, plan_hbm, block, cache, held, plan, chunks, kv, row, qf, of, lf, sems):
    rows = cache_copies(cache, kv, 0, sems, 0)
    small = [pltpu.make_async_copy(plan_hbm, plan, sems.at[2])]
    small.append(pltpu.make_async_copy(block, chunks, sems.at[3]))
    for copy in small + rows:
        copy.start()
    for copy in small:
        copy.wait()
    spread_queries(groups, [chunks.at[i] for i in range(SIDE)], qf, 0)
    attend_row(
        groups, block.shape[1], plan, kv.at[0], kv.at[1], rows[0].wait, rows[1].wait, row, qf, 0, of, lf
    )
    out = row_copy(row, held, 0, sems.at[4])
    out.start()
    out.wait()


def attend_others(groups, shifts, plan_hbm, *refs):
    count = len(shifts)
    given = refs[:count]
    cache, held_in, held, plan, blocks, kv, row, qf, of, lf, sems = refs[count:]
    ranges = given[0].shape[1]
    size = SIDE * groups * ranges
    small = [pltpu.make_async_copy(plan_hbm, plan, sems.at[0])]
    for i, block in enumerate(given):
        small.append(pltpu.make_async_copy(block, blocks.at[i], sems.at[1 + i]))
    rows = [
        cache_copies(cache, kv.at[i], k, sems, 1 + count + 2 * i) for i, k in enumerate(shifts)
    ]
    for copy in small + sum(rows, []):
        copy.start()
    for copy in small:
        copy.wait()
    for i in range(count):
        spread_queries(groups, [blocks.at[i, j] for j in range(SIDE)], qf, i * size)
    out = 1 + 3 * count

    def one(i, carry):
        def wait(w):
            for k in range(count):

                @pl.when(i == k)
                def _():
                    rows[k][w].wait()

        wait_k, wait_v = functools.partial(wait, 0), functools.partial(wait, 1)
        keys, values = kv.at[i, 0], kv.at[i, 1]
        base = pl.multiple_of(i * size, size)
        attend_row(groups, ranges, plan, keys, values, wait_k, wait_v, row.at[i], qf, base, of, lf)
        shift = jnp.where(i == 0, shifts[0], shifts[-1])
        row_copy(row.at[i], held, shift, sems.at[out + i]).start()
        return carry

    lax.fori_loop(0, count, one, 0)
    for i, shift in enumerate(shifts):
        row_copy(row.at[i], held, shift, sems.at[out + i]).wait()


def merge_sources(groups, put_ref, in_ref, out_ref, stage):
    sources, ranges = in_ref.shape[0], in_ref.shape[1]
    slots = out_ref.shape[0] // PAD
    lane = iota((ranges, HEAD_DIM), 1)
    lses = [join3(in_ref[i, :, groups * HEAD_DIM :], groups) for i in range(sources)]
    top = functools.reduce(jnp.maximum, lses)
    shares = [jnp.exp(l - top) for l in lses]
    total = functools.reduce(jnp.add, shares)
    lse = top + jnp.log(total)
    inverse = 1.0 / total
    shares = [s * inverse for s in shares]
    put = put_ref[...].astype(bf16)
    stats = jnp.zeros((ranges, HEAD_DIM), f32)
    for g in range(groups):
        cols = slice(g * HEAD_DIM, (g + 1) * HEAD_DIM)
        acc = jnp.zeros((ranges, HEAD_DIM), f32)
        for i in range(sources):
            acc = acc + shares[i][:, g : g + 1] * in_ref[i, :, cols].astype(f32)
        stage[pl.ds(g, slots, stride=PAD), :] = jnp.dot(
            put, acc.astype(bf16), preferred_element_type=f32
        )
        mine = (lane == g) | (lane == g + groups) | (lane == g + 2 * groups)
        stats = jnp.where(mine, jnp.broadcast_to(lse[:, g : g + 1], stats.shape), stats)
    parts = split3(stats, lane, groups)
    stage[pl.ds(groups, slots, stride=PAD), :] = jnp.dot(put, parts, preferred_element_type=f32)
    for g in range(groups + 1, PAD):
        stage[pl.ds(g, slots, stride=PAD), :] = jnp.zeros((slots, HEAD_DIM), f32)
    out_ref[...] = stage[...].astype(bf16)


def finish(steps, heads, in_ref, owner_ref, q_ref, k_ref, v_ref, out_ref, stage):
    groups = steps * heads
    lenders = in_ref.shape[0] // (CAP * PAD)
    scale = 1.0 / math.sqrt(HEAD_DIM)
    stage[...] = in_ref[...].astype(f32)

    def group(g):
        return jnp.concatenate(
            [stage[pl.ds(c * PAD + g, lenders, stride=CAP * PAD), :] for c in range(CAP)], axis=0
        )

    lses = jnp.transpose(join3(group(groups), groups), (1, 0))
    owned = owner_ref[...].astype(jnp.int32) == iota(owner_ref.shape, 0)
    keys = [k_ref[t].astype(f32) for t in range(steps)]
    values = [v_ref[t].astype(f32) for t in range(steps)]
    for s in range(steps):
        for h in range(heads):
            g = s * heads + h
            cols = slice(h * HEAD_DIM, (h + 1) * HEAD_DIM)
            q = q_ref[s, :, cols].astype(f32)
            scores = [
                jnp.sum(q * keys[t], axis=1, keepdims=True) * scale for t in range(s + 1)
            ]
            lent = jnp.where(owned, jnp.broadcast_to(lses[g : g + 1, :], owned.shape), VERY_LOW)
            top = functools.reduce(jnp.maximum, scores)
            top = jnp.maximum(top, jnp.max(lent, axis=1, keepdims=True))
            share = jnp.where(owned, jnp.exp(lent - top), 0.0)
            total = jnp.sum(share, axis=1, keepdims=True)
            acc = jnp.dot(
                share, group(g), preferred_element_type=f32, precision=lax.Precision.HIGHEST
            )
            for t in range(s + 1):
                weight = jnp.exp(scores[t] - top)
                total = total + weight
                acc = acc + weight.astype(bf16).astype(f32) * values[t]
            out_ref[s, :, cols] = (acc / total).astype(bf16)


def x_shift(k):
    return [(SIDE * y + x, SIDE * y + (x + k) % SIDE) for y in range(SIDE) for x in range(SIDE)]


def y_shift(k):
    return [(SIDE * y + x, SIDE * ((y + k) % SIDE) + x) for y in range(SIDE) for x in range(SIDE)]


def on_device(queries, new_kv, page_cache, range_owner, range_start, range_tokens):
    steps, requests, columns = queries.shape
    lenders = lax.axis_size("inst")
    tp_count = lax.axis_size("tp")
    my_tp = lax.axis_index("tp")
    pages, _, slice_tokens, kv_columns = page_cache.shape
    ranges = range_owner.shape[1]
    heads = columns // HEAD_DIM
    groups = steps * heads
    kv_heads = kv_columns // HEAD_DIM
    group_size = heads * tp_count // kv_heads
    slots = lenders * CAP
    wide = (groups + 1) * HEAD_DIM
    vmem = pl.BlockSpec(memory_space=pltpu.VMEM)
    smem = pl.BlockSpec(memory_space=pltpu.SMEM)
    hbm = pl.BlockSpec(memory_space=pltpu.HBM)
    params = pltpu.CompilerParams(vmem_limit_bytes=24 * 2**20)
    whole = pltpu.CompilerParams(vmem_limit_bytes=64 * 2**20 - 2**17)
    dma = pltpu.SemaphoreType.DMA

    sent, slot_owner = pl.pallas_call(
        prepare,
        in_specs=[hbm] * 2,
        out_specs=[vmem] * 2,
        out_shape=[
            jax.ShapeDtypeStruct((slots * groups, HEAD_DIM), bf16),
            jax.ShapeDtypeStruct((requests, slots), f32),
        ],
        scratch_shapes=[
            pltpu.VMEM(queries.shape, bf16),
            pltpu.VMEM(range_owner.shape, jnp.int32),
            pltpu.VMEM((slots * groups, HEAD_DIM), f32),
            dma((2,)),
        ],
        compiler_params=whole,
        name="prepare",
    )(queries, range_owner)
    got = lax.all_to_all(sent, "inst", split_axis=0, concat_axis=0, tiled=True)

    plan, pick, put = pl.pallas_call(
        functools.partial(make_plan, slice_tokens, pages),
        in_specs=[smem] * 3,
        out_specs=[smem, vmem, vmem],
        out_shape=[
            jax.ShapeDtypeStruct((8, ranges), jnp.int32),
            jax.ShapeDtypeStruct((ranges, slots), f32),
            jax.ShapeDtypeStruct((slots, ranges), f32),
        ],
        name="make_plan",
    )(range_owner, range_start, range_tokens)
    head = my_tp * heads // group_size
    fresh = lax.dynamic_slice_in_dim(new_kv, head * HEAD_DIM, HEAD_DIM, axis=3)

    own = pl.pallas_call(
        functools.partial(pick_ranges, groups),
        in_specs=[vmem] * 2,
        out_specs=vmem,
        out_shape=jax.ShapeDtypeStruct((ranges, groups * HEAD_DIM), bf16),
        scratch_shapes=[pltpu.VMEM((slots * groups, HEAD_DIM), f32)],
        compiler_params=params,
        name="pick_ranges",
    )(pick, got)
    block = jnp.stack([own] + [lax.ppermute(own, "tp", x_shift(k)) for k in SHIFTS])
    near = {k: lax.ppermute(block, "tp", y_shift(k)) for k in (1, SIDE - 1)}

    pair = 2 * HEAD_DIM
    size = SIDE * groups * ranges
    partial_type = jax.ShapeDtypeStruct((tp_count, ranges, wide), bf16)
    plan_type = pltpu.SMEM(plan.shape, jnp.int32)
    row_scratch = [pltpu.VMEM((size, HEAD_DIM), f32)] * 2
    partial = pl.pallas_call(
        functools.partial(attend_own, groups),
        in_specs=[hbm] * 3,
        out_specs=hbm,
        out_shape=partial_type,
        scratch_shapes=[
            plan_type,
            pltpu.VMEM((SIDE, ranges, groups * HEAD_DIM), bf16),
            pltpu.VMEM((2, pages, slice_tokens, pair), bf16),
            pltpu.VMEM((SIDE, ranges, wide), bf16),
            pltpu.VMEM((size, HEAD_DIM), f32),
        ]
        + row_scratch
        + [dma((5,))],
        compiler_params=whole,
        cost_estimate=pl.CostEstimate(flops=10**9, bytes_accessed=2**23, transcendentals=0),
        name="attend_own",
    )(plan, block, page_cache)
    passed, partial = lax.optimization_barrier((near[1], partial))
    far = lax.ppermute(passed, "tp", y_shift(1))
    for given in ({1: passed, SIDE - 1: near[SIDE - 1]}, {2: far}):
        count = len(given)
        partial = pl.pallas_call(
            functools.partial(attend_others, groups, list(given)),
            in_specs=[hbm] * (count + 3),
            out_specs=hbm,
            out_shape=partial_type,
            scratch_shapes=[
                plan_type,
                pltpu.VMEM((count, SIDE, ranges, groups * HEAD_DIM), bf16),
                pltpu.VMEM((count, 2, pages, slice_tokens, pair), bf16),
                pltpu.VMEM((count, SIDE, ranges, wide), bf16),
                pltpu.VMEM((count * size, HEAD_DIM), f32),
            ]
            + row_scratch
            + [dma((1 + 4 * count,))],
            input_output_aliases={count + 2: 0},
            compiler_params=whole,
            cost_estimate=pl.CostEstimate(
                flops=count * 10**9, bytes_accessed=count * 2**22, transcendentals=0
            ),
            name="attend_others",
        )(plan, *given.values(), page_cache, partial)

    parts = lax.all_to_all(partial, "tp", split_axis=0, concat_axis=0, tiled=True)
    lent = pl.pallas_call(
        functools.partial(merge_sources, groups),
        in_specs=[vmem] * 2,
        out_specs=vmem,
        out_shape=jax.ShapeDtypeStruct((slots * PAD, HEAD_DIM), bf16),
        scratch_shapes=[pltpu.VMEM((slots * PAD, HEAD_DIM), f32)],
        compiler_params=params,
        name="merge_sources",
    )(put, parts)
    back = lax.all_to_all(lent, "inst", split_axis=0, concat_axis=0, tiled=True)
    return pl.pallas_call(
        functools.partial(finish, steps, heads),
        in_specs=[vmem] * 5,
        out_specs=vmem,
        out_shape=jax.ShapeDtypeStruct((steps, requests, columns), bf16),
        scratch_shapes=[pltpu.VMEM((slots * PAD, HEAD_DIM), f32)],
        compiler_params=params,
        name="finish",
    )(back, slot_owner, queries, fresh[:, :, 0], fresh[:, :, 1])


def solution(mesh):
    placed = (
        P(None, "inst", "tp"),
        P(None, "inst", None, None),
        P("inst", None, "tp", None),
        P(),
        P(),
        P(),
    )
    return jax.shard_map(
        on_device, mesh=mesh, in_specs=placed, out_specs=P(None, "inst", "tp"), check_vma=False
    )
```

```python
import functools
import math

import jax
import jax.numpy as jnp
from jax import lax
from jax.experimental import pallas as pl
from jax.experimental.pallas import tpu as pltpu
from jax.sharding import PartitionSpec as P

HEAD_DIM = 128
PAGE = 256
CAP = 2
REQ_INST = 8
SIDE = 4
SHIFTS = (1, 3, 2)
FIRST = 8
CHUNK = 16
MORE = 8
FEW = 2
VERY_LOW = -1e30
FLOOR = -1e29
PAD = 16
PAGE_ROW, LOW_ROW, HIGH_ROW, RANGE_ROW, END_ROW, COUNT_ROW, START_ROW = range(7)

f32 = jnp.float32
bf16 = jnp.bfloat16


def iota(shape, dim):
    return lax.broadcasted_iota(jnp.int32, shape, dim)


def split3(stats, lane, groups):
    high = stats.astype(bf16).astype(f32)
    rest = stats - high
    mid = rest.astype(bf16).astype(f32)
    low = rest - mid
    return jnp.where(lane < groups, high, jnp.where(lane < 2 * groups, mid, low)).astype(bf16)


def join3(parts, groups):
    parts = parts.astype(f32)
    return (
        parts
        + pltpu.roll(parts, HEAD_DIM - groups, 1)
        + pltpu.roll(parts, HEAD_DIM - 2 * groups, 1)
    )


def prepare(q_hbm, owner_hbm, sent_ref, mine_ref, q_ref, owner_ref, stage, sems):
    copies = [
        pltpu.make_async_copy(owner_hbm, owner_ref, sems.at[0]),
        pltpu.make_async_copy(q_hbm, q_ref, sems.at[1]),
    ]
    for copy in copies:
        copy.start()
    steps, requests, columns = q_ref.shape
    heads = columns // HEAD_DIM
    groups = steps * heads
    lenders, ranges = owner_ref.shape
    earlier = (iota((ranges, ranges), 0) < iota((ranges, ranges), 1)).astype(f32)
    copies[0].wait()
    owner = owner_ref[...]
    hit = owner // REQ_INST == lax.axis_index("inst")
    rank = jnp.dot(hit.astype(f32), earlier, preferred_element_type=f32)
    local = (owner % REQ_INST + 1).astype(f32)
    owners = []
    for c in range(CAP):
        chosen = jnp.where(hit & (jnp.abs(rank - c) < 0.5), local, 0.0)
        owners.append(jnp.sum(chosen, axis=1, keepdims=True) - 1.0)
    copies[1].wait()
    for c in range(CAP):
        pick = (owners[c].astype(jnp.int32) == iota((lenders, requests), 1)).astype(f32)
        for s in range(steps):
            value = jnp.dot(pick, q_ref[s].astype(f32), preferred_element_type=f32)
            for h in range(heads):
                at = pl.ds(c * groups + s * heads + h, lenders, stride=CAP * groups)
                stage[at, :] = value[:, h * HEAD_DIM : (h + 1) * HEAD_DIM]
    sent_ref[...] = stage[...].astype(bf16)
    spread = [jnp.broadcast_to(mine, (lenders, HEAD_DIM)) for mine in owners]
    mine_ref[...] = jnp.transpose(jnp.concatenate(spread, axis=0), (1, 0))[: mine_ref.shape[0], :]


def make_plan(slice_tokens, pages, owner_ref, start_ref, tokens_ref, plan, pick_ref, put_ref):
    ranges = owner_ref.shape[1]
    me = lax.axis_index("inst")
    my_tp = lax.axis_index("tp")
    for i in range(RANGE_ROW + 1):
        for r in range(ranges):
            plan[i, r] = 0

    def fill(r, count):
        start = start_ref[me, r]
        tokens = tokens_ref[me, r]
        span = (tokens + PAGE - 1) // PAGE
        more = jnp.maximum(span - FIRST + CHUNK - 1, 0) // CHUNK
        tail = jnp.clip(tokens % PAGE - my_tp * slice_tokens, 0, slice_tokens)
        high = (start + tokens // PAGE) * slice_tokens + tail
        plan[END_ROW, r] = high
        plan[START_ROW, r] = start

        def one(j, carry):
            first = start + FIRST + j * CHUNK
            plan[PAGE_ROW, count + j] = jnp.minimum(first, pages - CHUNK)
            plan[LOW_ROW, count + j] = first * slice_tokens
            plan[HIGH_ROW, count + j] = high
            plan[RANGE_ROW, count + j] = r
            return carry

        lax.fori_loop(0, more, one, 0)
        return count + more

    plan[COUNT_ROW, 0] = lax.fori_loop(0, ranges, fill, 0)
    homes = [owner_ref[me, r] // REQ_INST for r in range(ranges)]
    pick = jnp.zeros(pick_ref.shape, f32)
    put = jnp.zeros(put_ref.shape, f32)
    for r in range(ranges):
        rank = sum([(homes[e] == homes[r]).astype(jnp.int32) for e in range(r)], jnp.int32(0))
        slot = homes[r] * CAP + rank
        pick = jnp.where((iota(pick.shape, 0) == r) & (iota(pick.shape, 1) == slot), 1.0, pick)
        put = jnp.where((iota(put.shape, 1) == r) & (iota(put.shape, 0) == slot), 1.0, put)
    pick_ref[...] = pick
    put_ref[...] = put


def pick_ranges(groups, pick_ref, got_ref, out_ref, stage):
    slots = got_ref.shape[0] // groups
    stage[...] = got_ref[...].astype(f32)
    pick = pick_ref[...]
    for g in range(groups):
        value = stage[pl.ds(g, slots, stride=groups), :]
        out_ref[:, g * HEAD_DIM : (g + 1) * HEAD_DIM] = jnp.dot(
            pick, value, preferred_element_type=f32
        ).astype(bf16)


def place_before(shift):
    return (lax.axis_index("tp") // SIDE + SIDE - shift) % SIDE


def spread_queries(groups, chunks, qf, base):
    ranges = chunks[0].shape[0]
    for k, chunk in zip((0,) + SHIFTS, chunks):
        x = (lax.axis_index("tp") + SIDE - k) % SIDE
        at = pl.multiple_of(x * (groups * ranges) + base, groups * ranges)
        for g in range(groups):
            cols = slice(g * HEAD_DIM, (g + 1) * HEAD_DIM)
            qf[pl.ds(at + g * ranges, ranges), :] = chunk[:, cols].astype(f32)


def attend_row(groups, ranges, plan, k_ref, v_ref, wait_k, wait_v, out_ref, qf, base, of, lf):
    rows = SIDE * groups
    half = rows // 2
    pages, slice_tokens, pair = k_ref.shape
    scale = 1.0 / math.sqrt(HEAD_DIM)
    exp2_scale = scale * math.log2(math.e)
    top = iota((rows, HEAD_DIM), 0) < half

    def load(ref, page, span):
        return ref[pl.ds(page, span)].reshape(span * slice_tokens, pair)

    def scores(span, r, page, low, high):
        q = qf[pl.ds(base + r, rows, stride=ranges), :]
        zero = jnp.zeros_like(q)
        wide = jnp.concatenate(
            [jnp.where(top, q, zero), jnp.where(top, zero, q)], axis=1
        ).astype(bf16)
        k = load(k_ref, page, span)
        s = lax.dot_general(wide, k, (((1,), (1,)), ((), ())), preferred_element_type=f32)
        at = iota((1, span * slice_tokens), 1) + page * slice_tokens
        return s + jnp.where((at >= low) & (at < high), 0.0, VERY_LOW)

    def softmax(s):
        m = jnp.maximum(jnp.max(s, axis=1, keepdims=True), FLOOR)
        p = jnp.exp2((s - m) * exp2_scale)
        total = jnp.sum(p, axis=1, keepdims=True)
        some = total > 0.0
        safe = jnp.where(some, total, 1.0)
        lse = jnp.where(some, m * scale + jnp.log(safe), VERY_LOW)
        return p.astype(bf16), 1.0 / safe, jnp.broadcast_to(lse, (rows, HEAD_DIM))

    def values(span, page, p, inverse):
        o = jnp.dot(p, load(v_ref, page, span), preferred_element_type=f32)
        return jnp.where(top, o[:, :HEAD_DIM], o[:, HEAD_DIM:]) * inverse

    def many(span, work, wait=None):
        s = [scores(span, *w) for w in work]
        s = [softmax(one) for one in s]
        if wait is not None:
            wait()
        o = [values(span, w[1], one[0], one[1]) for one, w in zip(s, work)]
        return [(one, lse) for one, (_, _, lse) in zip(o, s)]

    def place(r):
        return pl.ds(pl.multiple_of(r * rows, 8), rows)

    work = []
    for r in range(ranges):
        start = plan[START_ROW, r]
        page = jnp.minimum(start, pages - FIRST)
        work.append((r, page, start * slice_tokens, plan[END_ROW, r]))
    wait_k()
    for w, (o, lse) in zip(work, many(FIRST, work, wait_v)):
        of[place(w[0]), :] = o
        lf[place(w[0]), :] = lse

    def more(size, done, b, carry):
        work = []
        for j in range(size):
            e = done + b * size + j
            work.append((plan[RANGE_ROW, e], plan[PAGE_ROW, e], plan[LOW_ROW, e], plan[HIGH_ROW, e]))
        for w, (o, lse) in zip(work, many(CHUNK, work)):
            at = place(w[0])
            old = lf[at, :]
            high = jnp.maximum(old, lse)
            share_old = jnp.exp(old - high)
            share = jnp.exp(lse - high)
            total = share_old + share
            of[at, :] = (of[at, :] * share_old + o * share) / total
            lf[at, :] = high + jnp.log(total)
        return carry

    count = plan[COUNT_ROW, 0]
    large = (count + MORE // 2) // MORE
    done = large * MORE
    lax.fori_loop(0, large, functools.partial(more, MORE, 0), 0)
    rest = (jnp.maximum(count - done, 0) + FEW - 1) // FEW
    lax.fori_loop(0, rest, functools.partial(more, FEW, done), 0)

    lanes = iota((ranges, HEAD_DIM), 1)
    for x in range(SIDE):
        lse = jnp.zeros((ranges, HEAD_DIM), f32)
        for g in range(groups):
            at = pl.ds(x * groups + g, ranges, stride=rows)
            out_ref[x, :, g * HEAD_DIM : (g + 1) * HEAD_DIM] = of[at, :].astype(bf16)
            mine = (lanes == g) | (lanes == g + groups) | (lanes == g + 2 * groups)
            lse = jnp.where(mine, lf[at, :], lse)
        out_ref[x, :, groups * HEAD_DIM :] = split3(lse, lanes, groups)


def cache_copies(cache, target, shift, sems, first):
    pair = target.shape[-1]
    y = place_before(shift)
    columns = pl.ds(pl.multiple_of(y * pair, pair), pair)
    return [
        pltpu.make_async_copy(cache.at[:, w, :, columns], target.at[w], sems.at[first + w])
        for w in range(2)
    ]


def row_copy(row, held, shift, sem):
    y = place_before(shift)
    return pltpu.make_async_copy(row, held.at[pl.ds(y * SIDE, SIDE)], sem)


def attend_own(groups, plan_hbm, block, cache, held, plan, chunks, kv, row, qf, of, lf, sems):
    rows = cache_copies(cache, kv, 0, sems, 0)
    small = [pltpu.make_async_copy(plan_hbm, plan, sems.at[2])]
    small.append(pltpu.make_async_copy(block, chunks, sems.at[3]))
    for copy in small + rows:
        copy.start()
    for copy in small:
        copy.wait()
    spread_queries(groups, [chunks.at[i] for i in range(SIDE)], qf, 0)
    attend_row(
        groups, block.shape[1], plan, kv.at[0], kv.at[1], rows[0].wait, rows[1].wait, row, qf, 0, of, lf
    )
    out = row_copy(row, held, 0, sems.at[4])
    out.start()
    out.wait()


def attend_others(groups, shifts, plan_hbm, *refs):
    count = len(shifts)
    given = refs[:count]
    cache, held_in, held, plan, blocks, kv, row, qf, of, lf, sems = refs[count:]
    ranges = given[0].shape[1]
    size = SIDE * groups * ranges
    small = [pltpu.make_async_copy(plan_hbm, plan, sems.at[0])]
    for i, block in enumerate(given):
        small.append(pltpu.make_async_copy(block, blocks.at[i], sems.at[1 + i]))
    rows = [
        cache_copies(cache, kv.at[i], k, sems, 1 + count + 2 * i) for i, k in enumerate(shifts)
    ]
    for copy in small + rows[0]:
        copy.start()
    for copy in small:
        copy.wait()
    for i in range(count):
        spread_queries(groups, [blocks.at[i, j] for j in range(SIDE)], qf, i * size)
    out = 1 + 3 * count

    def one(i, carry):
        def wait(w):
            for k in range(count):

                @pl.when(i == k)
                def _():
                    rows[k][w].wait()
                    if w == 0 and k + 1 < count:
                        for copy in rows[k + 1]:
                            copy.start()

        wait_k, wait_v = functools.partial(wait, 0), functools.partial(wait, 1)
        keys, values = kv.at[i, 0], kv.at[i, 1]
        base = pl.multiple_of(i * size, size)
        attend_row(groups, ranges, plan, keys, values, wait_k, wait_v, row.at[i], qf, base, of, lf)
        shift = jnp.where(i == 0, shifts[0], shifts[-1])
        row_copy(row.at[i], held, shift, sems.at[out + i]).start()
        return carry

    lax.fori_loop(0, count, one, 0)
    for i, shift in enumerate(shifts):
        row_copy(row.at[i], held, shift, sems.at[out + i]).wait()


def merge_sources(groups, put_ref, in_ref, out_ref, stage):
    sources, ranges = in_ref.shape[0], in_ref.shape[1]
    slots = out_ref.shape[0] // PAD
    lane = iota((ranges, HEAD_DIM), 1)
    lses = [join3(in_ref[i, :, groups * HEAD_DIM :], groups) for i in range(sources)]
    top = functools.reduce(jnp.maximum, lses)
    shares = [jnp.exp(l - top) for l in lses]
    total = functools.reduce(jnp.add, shares)
    lse = top + jnp.log(total)
    inverse = 1.0 / total
    shares = [s * inverse for s in shares]
    put = put_ref[...].astype(bf16)
    for g in range(groups):
        cols = slice(g * HEAD_DIM, (g + 1) * HEAD_DIM)
        acc = jnp.zeros((ranges, HEAD_DIM), f32)
        for i in range(sources):
            acc = acc + shares[i][:, g : g + 1] * in_ref[i, :, cols].astype(f32)
        stage[pl.ds(g, slots, stride=PAD), :] = jnp.dot(
            put, acc.astype(bf16), preferred_element_type=f32
        )
    second, third = pltpu.roll(lse, groups, 1), pltpu.roll(lse, 2 * groups, 1)
    stats = jnp.where(lane < groups, lse, jnp.where(lane < 2 * groups, second, third))
    parts = split3(stats, lane, groups)
    stage[pl.ds(groups, slots, stride=PAD), :] = jnp.dot(put, parts, preferred_element_type=f32)
    for g in range(groups + 1, PAD):
        stage[pl.ds(g, slots, stride=PAD), :] = jnp.zeros((slots, HEAD_DIM), f32)
    out_ref[...] = stage[...].astype(bf16)


def finish(steps, heads, in_ref, owner_ref, q_ref, k_ref, v_ref, out_ref, stage):
    groups = steps * heads
    lenders = in_ref.shape[0] // (CAP * PAD)
    scale = 1.0 / math.sqrt(HEAD_DIM)
    stage[...] = in_ref[...].astype(f32)

    def group(g):
        return jnp.concatenate(
            [stage[pl.ds(c * PAD + g, lenders, stride=CAP * PAD), :] for c in range(CAP)], axis=0
        )

    lses = jnp.transpose(join3(group(groups), groups), (1, 0))
    owned = owner_ref[...].astype(jnp.int32) == iota(owner_ref.shape, 0)
    keys = [k_ref[t].astype(f32) for t in range(steps)]
    values = [v_ref[t].astype(f32) for t in range(steps)]
    for s in range(steps):
        for h in range(heads):
            g = s * heads + h
            cols = slice(h * HEAD_DIM, (h + 1) * HEAD_DIM)
            q = q_ref[s, :, cols].astype(f32)
            scores = [
                jnp.sum(q * keys[t], axis=1, keepdims=True) * scale for t in range(s + 1)
            ]
            lent = jnp.where(owned, jnp.broadcast_to(lses[g : g + 1, :], owned.shape), VERY_LOW)
            top = functools.reduce(jnp.maximum, scores)
            top = jnp.maximum(top, jnp.max(lent, axis=1, keepdims=True))
            share = jnp.where(owned, jnp.exp(lent - top), 0.0)
            total = jnp.sum(share, axis=1, keepdims=True)
            high = share.astype(bf16).astype(f32)
            parts = jnp.concatenate([high, share - high], axis=0).astype(bf16)
            sums = jnp.dot(parts, group(g).astype(bf16), preferred_element_type=f32)
            acc = sums[: len(share)] + sums[len(share) :]
            for t in range(s + 1):
                weight = jnp.exp(scores[t] - top)
                total = total + weight
                acc = acc + weight.astype(bf16).astype(f32) * values[t]
            out_ref[s, :, cols] = (acc / total).astype(bf16)


def x_shift(k):
    return [(SIDE * y + x, SIDE * y + (x + k) % SIDE) for y in range(SIDE) for x in range(SIDE)]


def y_shift(k):
    return [(SIDE * y + x, SIDE * ((y + k) % SIDE) + x) for y in range(SIDE) for x in range(SIDE)]


def on_device(queries, new_kv, page_cache, range_owner, range_start, range_tokens):
    steps, requests, columns = queries.shape
    lenders = lax.axis_size("inst")
    tp_count = lax.axis_size("tp")
    my_tp = lax.axis_index("tp")
    pages, _, slice_tokens, kv_columns = page_cache.shape
    ranges = range_owner.shape[1]
    heads = columns // HEAD_DIM
    groups = steps * heads
    kv_heads = kv_columns // HEAD_DIM
    group_size = heads * tp_count // kv_heads
    slots = lenders * CAP
    wide = (groups + 1) * HEAD_DIM
    vmem = pl.BlockSpec(memory_space=pltpu.VMEM)
    smem = pl.BlockSpec(memory_space=pltpu.SMEM)
    hbm = pl.BlockSpec(memory_space=pltpu.HBM)
    params = pltpu.CompilerParams(vmem_limit_bytes=24 * 2**20)
    grant = pltpu.CompilerParams(vmem_limit_bytes=57 * 2**20)
    whole = pltpu.CompilerParams(vmem_limit_bytes=64 * 2**20 - 2**17)
    dma = pltpu.SemaphoreType.DMA

    sent, slot_owner = pl.pallas_call(
        prepare,
        in_specs=[hbm] * 2,
        out_specs=[vmem] * 2,
        out_shape=[
            jax.ShapeDtypeStruct((slots * groups, HEAD_DIM), bf16),
            jax.ShapeDtypeStruct((requests, slots), f32),
        ],
        scratch_shapes=[
            pltpu.VMEM(queries.shape, bf16),
            pltpu.VMEM(range_owner.shape, jnp.int32),
            pltpu.VMEM((slots * groups, HEAD_DIM), f32),
            dma((2,)),
        ],
        compiler_params=whole,
        name="prepare",
    )(queries, range_owner)
    got = lax.all_to_all(sent, "inst", split_axis=0, concat_axis=0, tiled=True)

    plan, pick, put = pl.pallas_call(
        functools.partial(make_plan, slice_tokens, pages),
        in_specs=[smem] * 3,
        out_specs=[smem, vmem, vmem],
        out_shape=[
            jax.ShapeDtypeStruct((8, ranges), jnp.int32),
            jax.ShapeDtypeStruct((ranges, slots), f32),
            jax.ShapeDtypeStruct((slots, ranges), f32),
        ],
        compiler_params=params,
        name="make_plan",
    )(range_owner, range_start, range_tokens)
    head = my_tp * heads // group_size
    fresh = lax.dynamic_slice_in_dim(new_kv, head * HEAD_DIM, HEAD_DIM, axis=3)

    own = pl.pallas_call(
        functools.partial(pick_ranges, groups),
        in_specs=[vmem] * 2,
        out_specs=vmem,
        out_shape=jax.ShapeDtypeStruct((ranges, groups * HEAD_DIM), bf16),
        scratch_shapes=[pltpu.VMEM((slots * groups, HEAD_DIM), f32)],
        compiler_params=params,
        name="pick_ranges",
    )(pick, got)
    block = jnp.stack([own] + [lax.ppermute(own, "tp", x_shift(k)) for k in SHIFTS])
    near = {k: lax.ppermute(block, "tp", y_shift(k)) for k in (1, SIDE - 1)}

    pair = 2 * HEAD_DIM
    size = SIDE * groups * ranges
    partial_type = jax.ShapeDtypeStruct((tp_count, ranges, wide), bf16)
    plan_type = pltpu.SMEM(plan.shape, jnp.int32)
    row_scratch = [pltpu.VMEM((size, HEAD_DIM), f32)] * 2
    partial = pl.pallas_call(
        functools.partial(attend_own, groups),
        in_specs=[hbm] * 3,
        out_specs=hbm,
        out_shape=partial_type,
        scratch_shapes=[
            plan_type,
            pltpu.VMEM((SIDE, ranges, groups * HEAD_DIM), bf16),
            pltpu.VMEM((2, pages, slice_tokens, pair), bf16),
            pltpu.VMEM((SIDE, ranges, wide), bf16),
            pltpu.VMEM((size, HEAD_DIM), f32),
        ]
        + row_scratch
        + [dma((5,))],
        compiler_params=grant,
        cost_estimate=pl.CostEstimate(flops=10**9, bytes_accessed=2**23, transcendentals=0),
        name="attend_own",
    )(plan, block, page_cache)
    passed, partial = lax.optimization_barrier((near[1], partial))
    far = lax.ppermute(passed, "tp", y_shift(1))
    for given in ({1: passed, SIDE - 1: near[SIDE - 1]}, {2: far}):
        count = len(given)
        partial = pl.pallas_call(
            functools.partial(attend_others, groups, list(given)),
            in_specs=[hbm] * (count + 3),
            out_specs=hbm,
            out_shape=partial_type,
            scratch_shapes=[
                plan_type,
                pltpu.VMEM((count, SIDE, ranges, groups * HEAD_DIM), bf16),
                pltpu.VMEM((count, 2, pages, slice_tokens, pair), bf16),
                pltpu.VMEM((count, SIDE, ranges, wide), bf16),
                pltpu.VMEM((count * size, HEAD_DIM), f32),
            ]
            + row_scratch
            + [dma((1 + 4 * count,))],
            input_output_aliases={count + 2: 0},
            compiler_params=whole,
            cost_estimate=pl.CostEstimate(
                flops=count * 10**9, bytes_accessed=count * 2**22, transcendentals=0
            ),
            name="attend_others",
        )(plan, *given.values(), page_cache, partial)

    parts = lax.all_to_all(partial, "tp", split_axis=0, concat_axis=0, tiled=True)
    lent = pl.pallas_call(
        functools.partial(merge_sources, groups),
        in_specs=[vmem] * 2,
        out_specs=vmem,
        out_shape=jax.ShapeDtypeStruct((slots * PAD, HEAD_DIM), bf16),
        scratch_shapes=[pltpu.VMEM((slots * PAD, HEAD_DIM), f32)],
        compiler_params=params,
        name="merge_sources",
    )(put, parts)
    back = lax.all_to_all(lent, "inst", split_axis=0, concat_axis=0, tiled=True)
    return pl.pallas_call(
        functools.partial(finish, steps, heads),
        in_specs=[vmem] * 5,
        out_specs=vmem,
        out_shape=jax.ShapeDtypeStruct((steps, requests, columns), bf16),
        scratch_shapes=[pltpu.VMEM((slots * PAD, HEAD_DIM), f32)],
        compiler_params=params,
        name="finish",
    )(back, slot_owner, queries, fresh[:, :, 0], fresh[:, :, 1])


def solution(mesh):
    placed = (
        P(None, "inst", "tp"),
        P(None, "inst", None, None),
        P("inst", None, "tp", None),
        P(),
        P(),
        P(),
    )
    return jax.shard_map(
        on_device, mesh=mesh, in_specs=placed, out_specs=P(None, "inst", "tp"), check_vma=False
    )
```

```python
import functools
import math

import jax
import jax.numpy as jnp
from jax import lax
from jax.experimental import pallas as pl
from jax.experimental.pallas import tpu as pltpu
from jax.sharding import PartitionSpec as P

HEAD_DIM = 128
PAGE = 256
CAP = 2
REQ_INST = 8
SIDE = 4
SHIFTS = (1, 3, 2)
FIRST = 8
CHUNK = 16
MORE = 8
FEW = 2
VERY_LOW = -1e30
FLOOR = -1e29
PAD = 16
PAGE_ROW, LOW_ROW, HIGH_ROW, RANGE_ROW, END_ROW, COUNT_ROW, START_ROW = range(7)

f32 = jnp.float32
bf16 = jnp.bfloat16


def iota(shape, dim):
    return lax.broadcasted_iota(jnp.int32, shape, dim)


def split3(stats, lane, groups):
    high = stats.astype(bf16).astype(f32)
    rest = stats - high
    mid = rest.astype(bf16).astype(f32)
    low = rest - mid
    return jnp.where(lane < groups, high, jnp.where(lane < 2 * groups, mid, low)).astype(bf16)


def join3(parts, groups):
    parts = parts.astype(f32)
    return (
        parts
        + pltpu.roll(parts, HEAD_DIM - groups, 1)
        + pltpu.roll(parts, HEAD_DIM - 2 * groups, 1)
    )


def prepare(q_hbm, owner_hbm, sent_ref, mine_ref, q_ref, owner_ref, stage, sems):
    copies = [
        pltpu.make_async_copy(owner_hbm, owner_ref, sems.at[0]),
        pltpu.make_async_copy(q_hbm, q_ref, sems.at[1]),
    ]
    for copy in copies:
        copy.start()
    steps, requests, columns = q_ref.shape
    heads = columns // HEAD_DIM
    groups = steps * heads
    lenders, ranges = owner_ref.shape
    earlier = (iota((ranges, ranges), 0) < iota((ranges, ranges), 1)).astype(f32)
    copies[0].wait()
    owner = owner_ref[...]
    hit = owner // REQ_INST == lax.axis_index("inst")
    rank = jnp.dot(hit.astype(f32), earlier, preferred_element_type=f32)
    local = (owner % REQ_INST + 1).astype(f32)
    owners = []
    for c in range(CAP):
        chosen = jnp.where(hit & (jnp.abs(rank - c) < 0.5), local, 0.0)
        owners.append(jnp.sum(chosen, axis=1, keepdims=True) - 1.0)
    copies[1].wait()
    for c in range(CAP):
        pick = (owners[c].astype(jnp.int32) == iota((lenders, requests), 1)).astype(f32)
        for s in range(steps):
            value = jnp.dot(pick, q_ref[s].astype(f32), preferred_element_type=f32)
            for h in range(heads):
                at = pl.ds(c * groups + s * heads + h, lenders, stride=CAP * groups)
                stage[at, :] = value[:, h * HEAD_DIM : (h + 1) * HEAD_DIM]
    sent_ref[...] = stage[...].astype(bf16)
    spread = [jnp.broadcast_to(mine, (lenders, HEAD_DIM)) for mine in owners]
    mine_ref[...] = jnp.transpose(jnp.concatenate(spread, axis=0), (1, 0))[: mine_ref.shape[0], :]


def make_plan(slice_tokens, pages, owner_ref, start_ref, tokens_ref, plan, pick_ref, put_ref):
    ranges = owner_ref.shape[1]
    me = lax.axis_index("inst")
    my_tp = lax.axis_index("tp")
    for i in range(RANGE_ROW + 1):
        for r in range(ranges):
            plan[i, r] = 0

    def fill(r, count):
        start = start_ref[me, r]
        tokens = tokens_ref[me, r]
        span = (tokens + PAGE - 1) // PAGE
        more = jnp.maximum(span - FIRST + CHUNK - 1, 0) // CHUNK
        tail = jnp.clip(tokens % PAGE - my_tp * slice_tokens, 0, slice_tokens)
        high = (start + tokens // PAGE) * slice_tokens + tail
        plan[END_ROW, r] = high
        plan[START_ROW, r] = start

        def one(j, carry):
            first = start + FIRST + j * CHUNK
            plan[PAGE_ROW, count + j] = jnp.minimum(first, pages - CHUNK)
            plan[LOW_ROW, count + j] = first * slice_tokens
            plan[HIGH_ROW, count + j] = high
            plan[RANGE_ROW, count + j] = r
            return carry

        lax.fori_loop(0, more, one, 0)
        return count + more

    plan[COUNT_ROW, 0] = lax.fori_loop(0, ranges, fill, 0)
    homes = [owner_ref[me, r] // REQ_INST for r in range(ranges)]
    pick = jnp.zeros(pick_ref.shape, f32)
    put = jnp.zeros(put_ref.shape, f32)
    for r in range(ranges):
        rank = sum([(homes[e] == homes[r]).astype(jnp.int32) for e in range(r)], jnp.int32(0))
        slot = homes[r] * CAP + rank
        pick = jnp.where((iota(pick.shape, 0) == r) & (iota(pick.shape, 1) == slot), 1.0, pick)
        put = jnp.where((iota(put.shape, 1) == r) & (iota(put.shape, 0) == slot), 1.0, put)
    pick_ref[...] = pick
    put_ref[...] = put


def pick_ranges(groups, pick_ref, got_ref, out_ref, stage):
    slots = got_ref.shape[0] // groups
    stage[...] = got_ref[...].astype(f32)
    pick = pick_ref[...]
    for g in range(groups):
        value = stage[pl.ds(g, slots, stride=groups), :]
        out_ref[:, g * HEAD_DIM : (g + 1) * HEAD_DIM] = jnp.dot(
            pick, value, preferred_element_type=f32
        ).astype(bf16)


def place_before(shift):
    return (lax.axis_index("tp") // SIDE + SIDE - shift) % SIDE


def spread_queries(groups, chunks, qf, base):
    ranges = chunks[0].shape[0]
    for k, chunk in zip((0,) + SHIFTS, chunks):
        x = (lax.axis_index("tp") + SIDE - k) % SIDE
        at = pl.multiple_of(x * (groups * ranges) + base, groups * ranges)
        for g in range(groups):
            cols = slice(g * HEAD_DIM, (g + 1) * HEAD_DIM)
            qf[pl.ds(at + g * ranges, ranges), :] = chunk[:, cols].astype(f32)


def attend_row(groups, ranges, plan, k_ref, v_ref, wait_k, wait_v, out_ref, qf, base, of, lf):
    rows = SIDE * groups
    half = rows // 2
    pages, slice_tokens, pair = k_ref.shape
    scale = 1.0 / math.sqrt(HEAD_DIM)
    exp2_scale = scale * math.log2(math.e)
    top = iota((rows, HEAD_DIM), 0) < half

    def load(ref, page, span):
        return ref[pl.ds(page, span)].reshape(span * slice_tokens, pair)

    def scores(span, r, page, low, high):
        q = qf[pl.ds(base + r, rows, stride=ranges), :]
        zero = jnp.zeros_like(q)
        wide = jnp.concatenate(
            [jnp.where(top, q, zero), jnp.where(top, zero, q)], axis=1
        ).astype(bf16)
        k = load(k_ref, page, span)
        s = lax.dot_general(wide, k, (((1,), (1,)), ((), ())), preferred_element_type=f32)
        at = iota((1, span * slice_tokens), 1) + page * slice_tokens
        return s + jnp.where((at >= low) & (at < high), 0.0, VERY_LOW)

    def softmax(s):
        m = jnp.maximum(jnp.max(s, axis=1, keepdims=True), FLOOR)
        p = jnp.exp2((s - m) * exp2_scale)
        total = jnp.sum(p, axis=1, keepdims=True)
        some = total > 0.0
        safe = jnp.where(some, total, 1.0)
        lse = jnp.where(some, m * scale + jnp.log(safe), VERY_LOW)
        return p.astype(bf16), 1.0 / safe, jnp.broadcast_to(lse, (rows, HEAD_DIM))

    def values(span, page, p, inverse):
        o = jnp.dot(p, load(v_ref, page, span), preferred_element_type=f32)
        return jnp.where(top, o[:, :HEAD_DIM], o[:, HEAD_DIM:]) * inverse

    def place(r):
        return pl.ds(pl.multiple_of(r * rows, 8), rows)

    def later(e):
        return plan[RANGE_ROW, e], plan[PAGE_ROW, e], plan[LOW_ROW, e], plan[HIGH_ROW, e]

    def join(r, o, lse):
        at = place(r)
        old = lf[at, :]
        high = jnp.maximum(old, lse)
        share_old = jnp.exp(old - high)
        share = jnp.exp(lse - high)
        total = share_old + share
        of[at, :] = (of[at, :] * share_old + o * share) / total
        lf[at, :] = high + jnp.log(total)

    work = []
    for r in range(ranges):
        start = plan[START_ROW, r]
        page = jnp.minimum(start, pages - FIRST)
        work.append((FIRST, r, page, start * slice_tokens, plan[END_ROW, r]))
    for e in range(MORE):
        work.append((CHUNK, *later(e)))
    wait_k()
    parts = [scores(*w) for w in work]
    parts = [softmax(one) for one in parts]
    wait_v()
    outs = [values(w[0], w[2], p[0], p[1]) for p, w in zip(parts, work)]

    for w, (_, _, lse), o in zip(work[:ranges], parts, outs):
        of[place(w[1]), :] = o
        lf[place(w[1]), :] = lse
    for w, (_, _, lse), o in zip(work[ranges:], parts[ranges:], outs[ranges:]):
        join(w[1], o, lse)

    def few(b, carry):
        work = [later(MORE + b * FEW + j) for j in range(FEW)]
        parts = [softmax(scores(CHUNK, *w)) for w in work]
        outs = [values(CHUNK, w[1], p[0], p[1]) for p, w in zip(parts, work)]
        for w, (_, _, lse), o in zip(work, parts, outs):
            join(w[0], o, lse)
        return carry

    lax.fori_loop(0, (jnp.maximum(plan[COUNT_ROW, 0] - MORE, 0) + FEW - 1) // FEW, few, 0)

    lanes = iota((ranges, HEAD_DIM), 1)
    for x in range(SIDE):
        lse = jnp.zeros((ranges, HEAD_DIM), f32)
        for g in range(groups):
            at = pl.ds(x * groups + g, ranges, stride=rows)
            out_ref[x, :, g * HEAD_DIM : (g + 1) * HEAD_DIM] = of[at, :].astype(bf16)
            mine = (lanes == g) | (lanes == g + groups) | (lanes == g + 2 * groups)
            lse = jnp.where(mine, lf[at, :], lse)
        out_ref[x, :, groups * HEAD_DIM :] = split3(lse, lanes, groups)


def cache_copies(cache, target, shift, sems, first):
    pair = target.shape[-1]
    y = place_before(shift)
    columns = pl.ds(pl.multiple_of(y * pair, pair), pair)
    return [
        pltpu.make_async_copy(cache.at[:, w, :, columns], target.at[w], sems.at[first + w])
        for w in range(2)
    ]


def row_copy(row, held, shift, sem):
    y = place_before(shift)
    return pltpu.make_async_copy(row, held.at[pl.ds(y * SIDE, SIDE)], sem)


def attend_own(groups, plan_hbm, block, cache, held, plan, chunks, kv, row, qf, of, lf, sems):
    rows = cache_copies(cache, kv, 0, sems, 0)
    small = [pltpu.make_async_copy(plan_hbm, plan, sems.at[2])]
    small.append(pltpu.make_async_copy(block, chunks, sems.at[3]))
    for copy in small + rows:
        copy.start()
    for copy in small:
        copy.wait()
    spread_queries(groups, [chunks.at[i] for i in range(SIDE)], qf, 0)
    attend_row(
        groups, block.shape[1], plan, kv.at[0], kv.at[1], rows[0].wait, rows[1].wait, row, qf, 0, of, lf
    )
    out = row_copy(row, held, 0, sems.at[4])
    out.start()
    out.wait()


def attend_others(groups, shifts, plan_hbm, *refs):
    count = len(shifts)
    given = refs[:count]
    cache, held_in, held, plan, blocks, kv, row, qf, of, lf, sems = refs[count:]
    ranges = given[0].shape[1]
    size = SIDE * groups * ranges
    small = [pltpu.make_async_copy(plan_hbm, plan, sems.at[0])]
    for i, block in enumerate(given):
        small.append(pltpu.make_async_copy(block, blocks.at[i], sems.at[1 + i]))
    rows = [
        cache_copies(cache, kv.at[i], k, sems, 1 + count + 2 * i) for i, k in enumerate(shifts)
    ]
    for copy in small + rows[0]:
        copy.start()
    for copy in small:
        copy.wait()
    for i in range(count):
        spread_queries(groups, [blocks.at[i, j] for j in range(SIDE)], qf, i * size)
    out = 1 + 3 * count

    def one(i, carry):
        def wait(w):
            for k in range(count):

                @pl.when(i == k)
                def _():
                    rows[k][w].wait()
                    if w == 0 and k + 1 < count:
                        for copy in rows[k + 1]:
                            copy.start()

        wait_k, wait_v = functools.partial(wait, 0), functools.partial(wait, 1)
        keys, values = kv.at[i, 0], kv.at[i, 1]
        base = pl.multiple_of(i * size, size)
        attend_row(groups, ranges, plan, keys, values, wait_k, wait_v, row.at[i], qf, base, of, lf)
        shift = jnp.where(i == 0, shifts[0], shifts[-1])
        row_copy(row.at[i], held, shift, sems.at[out + i]).start()
        return carry

    lax.fori_loop(0, count, one, 0)
    for i, shift in enumerate(shifts):
        row_copy(row.at[i], held, shift, sems.at[out + i]).wait()


def merge_sources(groups, put_ref, in_ref, out_ref, stage):
    sources, ranges = in_ref.shape[0], in_ref.shape[1]
    slots = out_ref.shape[0] // PAD
    lane = iota((ranges, HEAD_DIM), 1)
    lses = [join3(in_ref[i, :, groups * HEAD_DIM :], groups) for i in range(sources)]
    top = functools.reduce(jnp.maximum, lses)
    shares = [jnp.exp(l - top) for l in lses]
    total = functools.reduce(jnp.add, shares)
    lse = top + jnp.log(total)
    inverse = 1.0 / total
    shares = [s * inverse for s in shares]
    put = put_ref[...].astype(bf16)
    for g in range(groups):
        cols = slice(g * HEAD_DIM, (g + 1) * HEAD_DIM)
        acc = jnp.zeros((ranges, HEAD_DIM), f32)
        for i in range(sources):
            acc = acc + shares[i][:, g : g + 1] * in_ref[i, :, cols].astype(f32)
        stage[pl.ds(g, slots, stride=PAD), :] = jnp.dot(
            put, acc.astype(bf16), preferred_element_type=f32
        )
    second, third = pltpu.roll(lse, groups, 1), pltpu.roll(lse, 2 * groups, 1)
    stats = jnp.where(lane < groups, lse, jnp.where(lane < 2 * groups, second, third))
    parts = split3(stats, lane, groups)
    stage[pl.ds(groups, slots, stride=PAD), :] = jnp.dot(put, parts, preferred_element_type=f32)
    for g in range(groups + 1, PAD):
        stage[pl.ds(g, slots, stride=PAD), :] = jnp.zeros((slots, HEAD_DIM), f32)
    out_ref[...] = stage[...].astype(bf16)


def finish(steps, heads, in_ref, owner_ref, q_ref, k_ref, v_ref, out_ref, stage):
    groups = steps * heads
    lenders = in_ref.shape[0] // (CAP * PAD)
    scale = 1.0 / math.sqrt(HEAD_DIM)
    stage[...] = in_ref[...].astype(f32)

    def group(g):
        return jnp.concatenate(
            [stage[pl.ds(c * PAD + g, lenders, stride=CAP * PAD), :] for c in range(CAP)], axis=0
        )

    lses = jnp.transpose(join3(group(groups), groups), (1, 0))
    owned = owner_ref[...].astype(jnp.int32) == iota(owner_ref.shape, 0)
    keys = [k_ref[t].astype(f32) for t in range(steps)]
    values = [v_ref[t].astype(f32) for t in range(steps)]
    for s in range(steps):
        for h in range(heads):
            g = s * heads + h
            cols = slice(h * HEAD_DIM, (h + 1) * HEAD_DIM)
            q = q_ref[s, :, cols].astype(f32)
            scores = [
                jnp.sum(q * keys[t], axis=1, keepdims=True) * scale for t in range(s + 1)
            ]
            lent = jnp.where(owned, jnp.broadcast_to(lses[g : g + 1, :], owned.shape), VERY_LOW)
            top = functools.reduce(jnp.maximum, scores)
            top = jnp.maximum(top, jnp.max(lent, axis=1, keepdims=True))
            share = jnp.where(owned, jnp.exp(lent - top), 0.0)
            total = jnp.sum(share, axis=1, keepdims=True)
            high = share.astype(bf16).astype(f32)
            parts = jnp.concatenate([high, share - high], axis=0).astype(bf16)
            sums = jnp.dot(parts, group(g).astype(bf16), preferred_element_type=f32)
            acc = sums[: len(share)] + sums[len(share) :]
            for t in range(s + 1):
                weight = jnp.exp(scores[t] - top)
                total = total + weight
                acc = acc + weight.astype(bf16).astype(f32) * values[t]
            out_ref[s, :, cols] = (acc / total).astype(bf16)


def x_shift(k):
    return [(SIDE * y + x, SIDE * y + (x + k) % SIDE) for y in range(SIDE) for x in range(SIDE)]


def y_shift(k):
    return [(SIDE * y + x, SIDE * ((y + k) % SIDE) + x) for y in range(SIDE) for x in range(SIDE)]


def on_device(queries, new_kv, page_cache, range_owner, range_start, range_tokens):
    steps, requests, columns = queries.shape
    lenders = lax.axis_size("inst")
    tp_count = lax.axis_size("tp")
    my_tp = lax.axis_index("tp")
    pages, _, slice_tokens, kv_columns = page_cache.shape
    ranges = range_owner.shape[1]
    heads = columns // HEAD_DIM
    groups = steps * heads
    kv_heads = kv_columns // HEAD_DIM
    group_size = heads * tp_count // kv_heads
    slots = lenders * CAP
    wide = (groups + 1) * HEAD_DIM
    vmem = pl.BlockSpec(memory_space=pltpu.VMEM)
    smem = pl.BlockSpec(memory_space=pltpu.SMEM)
    hbm = pl.BlockSpec(memory_space=pltpu.HBM)
    params = pltpu.CompilerParams(vmem_limit_bytes=24 * 2**20)
    grant = pltpu.CompilerParams(vmem_limit_bytes=57 * 2**20)
    whole = pltpu.CompilerParams(vmem_limit_bytes=64 * 2**20 - 2**17)
    dma = pltpu.SemaphoreType.DMA

    sent, slot_owner = pl.pallas_call(
        prepare,
        in_specs=[hbm] * 2,
        out_specs=[vmem] * 2,
        out_shape=[
            jax.ShapeDtypeStruct((slots * groups, HEAD_DIM), bf16),
            jax.ShapeDtypeStruct((requests, slots), f32),
        ],
        scratch_shapes=[
            pltpu.VMEM(queries.shape, bf16),
            pltpu.VMEM(range_owner.shape, jnp.int32),
            pltpu.VMEM((slots * groups, HEAD_DIM), f32),
            dma((2,)),
        ],
        compiler_params=whole,
        name="prepare",
    )(queries, range_owner)
    got = lax.all_to_all(sent, "inst", split_axis=0, concat_axis=0, tiled=True)

    plan, pick, put = pl.pallas_call(
        functools.partial(make_plan, slice_tokens, pages),
        in_specs=[smem] * 3,
        out_specs=[smem, vmem, vmem],
        out_shape=[
            jax.ShapeDtypeStruct((8, ranges), jnp.int32),
            jax.ShapeDtypeStruct((ranges, slots), f32),
            jax.ShapeDtypeStruct((slots, ranges), f32),
        ],
        compiler_params=params,
        name="make_plan",
    )(range_owner, range_start, range_tokens)
    head = my_tp * heads // group_size
    fresh = lax.dynamic_slice_in_dim(new_kv, head * HEAD_DIM, HEAD_DIM, axis=3)

    own = pl.pallas_call(
        functools.partial(pick_ranges, groups),
        in_specs=[vmem] * 2,
        out_specs=vmem,
        out_shape=jax.ShapeDtypeStruct((ranges, groups * HEAD_DIM), bf16),
        scratch_shapes=[pltpu.VMEM((slots * groups, HEAD_DIM), f32)],
        compiler_params=params,
        name="pick_ranges",
    )(pick, got)
    block = jnp.stack([own] + [lax.ppermute(own, "tp", x_shift(k)) for k in SHIFTS])
    near = {k: lax.ppermute(block, "tp", y_shift(k)) for k in (1, SIDE - 1)}

    pair = 2 * HEAD_DIM
    size = SIDE * groups * ranges
    partial_type = jax.ShapeDtypeStruct((tp_count, ranges, wide), bf16)
    plan_type = pltpu.SMEM(plan.shape, jnp.int32)
    row_scratch = [pltpu.VMEM((size, HEAD_DIM), f32)] * 2
    partial = pl.pallas_call(
        functools.partial(attend_own, groups),
        in_specs=[hbm] * 3,
        out_specs=hbm,
        out_shape=partial_type,
        scratch_shapes=[
            plan_type,
            pltpu.VMEM((SIDE, ranges, groups * HEAD_DIM), bf16),
            pltpu.VMEM((2, pages, slice_tokens, pair), bf16),
            pltpu.VMEM((SIDE, ranges, wide), bf16),
            pltpu.VMEM((size, HEAD_DIM), f32),
        ]
        + row_scratch
        + [dma((5,))],
        compiler_params=grant,
        cost_estimate=pl.CostEstimate(flops=10**9, bytes_accessed=2**23, transcendentals=0),
        name="attend_own",
    )(plan, block, page_cache)
    passed, partial = lax.optimization_barrier((near[1], partial))
    far = lax.ppermute(passed, "tp", y_shift(1))
    for given in ({1: passed, SIDE - 1: near[SIDE - 1]}, {2: far}):
        count = len(given)
        partial = pl.pallas_call(
            functools.partial(attend_others, groups, list(given)),
            in_specs=[hbm] * (count + 3),
            out_specs=hbm,
            out_shape=partial_type,
            scratch_shapes=[
                plan_type,
                pltpu.VMEM((count, SIDE, ranges, groups * HEAD_DIM), bf16),
                pltpu.VMEM((count, 2, pages, slice_tokens, pair), bf16),
                pltpu.VMEM((count, SIDE, ranges, wide), bf16),
                pltpu.VMEM((count * size, HEAD_DIM), f32),
            ]
            + row_scratch
            + [dma((1 + 4 * count,))],
            input_output_aliases={count + 2: 0},
            compiler_params=whole,
            cost_estimate=pl.CostEstimate(
                flops=count * 10**9, bytes_accessed=count * 2**22, transcendentals=0
            ),
            name="attend_others",
        )(plan, *given.values(), page_cache, partial)

    parts = lax.all_to_all(partial, "tp", split_axis=0, concat_axis=0, tiled=True)
    lent = pl.pallas_call(
        functools.partial(merge_sources, groups),
        in_specs=[vmem] * 2,
        out_specs=vmem,
        out_shape=jax.ShapeDtypeStruct((slots * PAD, HEAD_DIM), bf16),
        scratch_shapes=[pltpu.VMEM((slots * PAD, HEAD_DIM), f32)],
        compiler_params=params,
        name="merge_sources",
    )(put, parts)
    back = lax.all_to_all(lent, "inst", split_axis=0, concat_axis=0, tiled=True)
    return pl.pallas_call(
        functools.partial(finish, steps, heads),
        in_specs=[vmem] * 5,
        out_specs=vmem,
        out_shape=jax.ShapeDtypeStruct((steps, requests, columns), bf16),
        scratch_shapes=[pltpu.VMEM((slots * PAD, HEAD_DIM), f32)],
        compiler_params=params,
        name="finish",
    )(back, slot_owner, queries, fresh[:, :, 0], fresh[:, :, 1])


def solution(mesh):
    placed = (
        P(None, "inst", "tp"),
        P(None, "inst", None, None),
        P("inst", None, "tp", None),
        P(),
        P(),
        P(),
    )
    return jax.shard_map(
        on_device, mesh=mesh, in_specs=placed, out_specs=P(None, "inst", "tp"), check_vma=False
    )
```

```python
import functools
import math

import jax
import jax.numpy as jnp
from jax import lax
from jax.experimental import pallas as pl
from jax.experimental.pallas import tpu as pltpu
from jax.sharding import PartitionSpec as P

HEAD_DIM = 128
PAGE = 256
CAP = 2
REQ_INST = 8
SIDE = 4
SHIFTS = (1, 3, 2)
FIRST = 8
CHUNK = 16
MORE = 8
FEW = 2
VERY_LOW = -1e30
FLOOR = -1e29
PAD = 16
PAGE_ROW, LOW_ROW, HIGH_ROW, RANGE_ROW, END_ROW, COUNT_ROW, START_ROW = range(7)

f32 = jnp.float32
bf16 = jnp.bfloat16


def iota(shape, dim):
    return lax.broadcasted_iota(jnp.int32, shape, dim)


def split3(stats, lane, groups):
    high = stats.astype(bf16).astype(f32)
    rest = stats - high
    mid = rest.astype(bf16).astype(f32)
    low = rest - mid
    return jnp.where(lane < groups, high, jnp.where(lane < 2 * groups, mid, low)).astype(bf16)


def join3(parts, groups):
    parts = parts.astype(f32)
    return (
        parts
        + pltpu.roll(parts, HEAD_DIM - groups, 1)
        + pltpu.roll(parts, HEAD_DIM - 2 * groups, 1)
    )


def prepare(q_hbm, owner_hbm, sent_ref, mine_ref, q_ref, owner_ref, stage, sems):
    copies = [
        pltpu.make_async_copy(owner_hbm, owner_ref, sems.at[0]),
        pltpu.make_async_copy(q_hbm, q_ref, sems.at[1]),
    ]
    for copy in copies:
        copy.start()
    steps, requests, columns = q_ref.shape
    heads = columns // HEAD_DIM
    groups = steps * heads
    lenders, ranges = owner_ref.shape
    earlier = (iota((ranges, ranges), 0) < iota((ranges, ranges), 1)).astype(f32)
    copies[0].wait()
    owner = owner_ref[...]
    hit = owner // REQ_INST == lax.axis_index("inst")
    rank = jnp.dot(hit.astype(f32), earlier, preferred_element_type=f32)
    local = (owner % REQ_INST + 1).astype(f32)
    owners = []
    for c in range(CAP):
        chosen = jnp.where(hit & (jnp.abs(rank - c) < 0.5), local, 0.0)
        owners.append(jnp.sum(chosen, axis=1, keepdims=True) - 1.0)
    copies[1].wait()
    for c in range(CAP):
        pick = (owners[c].astype(jnp.int32) == iota((lenders, requests), 1)).astype(f32)
        for s in range(steps):
            value = jnp.dot(pick, q_ref[s].astype(f32), preferred_element_type=f32)
            for h in range(heads):
                at = pl.ds(c * groups + s * heads + h, lenders, stride=CAP * groups)
                stage[at, :] = value[:, h * HEAD_DIM : (h + 1) * HEAD_DIM]
    sent_ref[...] = stage[...].astype(bf16)
    spread = [jnp.broadcast_to(mine, (lenders, HEAD_DIM)) for mine in owners]
    mine_ref[...] = jnp.transpose(jnp.concatenate(spread, axis=0), (1, 0))[: mine_ref.shape[0], :]


def make_plan(slice_tokens, pages, owner_ref, start_ref, tokens_ref, plan, pick_ref, put_ref):
    ranges = owner_ref.shape[1]
    me = lax.axis_index("inst")
    my_tp = lax.axis_index("tp")
    for i in range(RANGE_ROW + 1):
        for r in range(ranges):
            plan[i, r] = 0

    def fill(r, count):
        start = start_ref[me, r]
        tokens = tokens_ref[me, r]
        span = (tokens + PAGE - 1) // PAGE
        more = jnp.maximum(span - FIRST + CHUNK - 1, 0) // CHUNK
        tail = jnp.clip(tokens % PAGE - my_tp * slice_tokens, 0, slice_tokens)
        high = (start + tokens // PAGE) * slice_tokens + tail
        plan[END_ROW, r] = high
        plan[START_ROW, r] = start

        def one(j, carry):
            first = start + FIRST + j * CHUNK
            plan[PAGE_ROW, count + j] = jnp.minimum(first, pages - CHUNK)
            plan[LOW_ROW, count + j] = first * slice_tokens
            plan[HIGH_ROW, count + j] = high
            plan[RANGE_ROW, count + j] = r
            return carry

        lax.fori_loop(0, more, one, 0)
        return count + more

    plan[COUNT_ROW, 0] = lax.fori_loop(0, ranges, fill, 0)
    homes = [owner_ref[me, r] // REQ_INST for r in range(ranges)]
    pick = jnp.zeros(pick_ref.shape, f32)
    put = jnp.zeros(put_ref.shape, f32)
    for r in range(ranges):
        rank = sum([(homes[e] == homes[r]).astype(jnp.int32) for e in range(r)], jnp.int32(0))
        slot = homes[r] * CAP + rank
        pick = jnp.where((iota(pick.shape, 0) == r) & (iota(pick.shape, 1) == slot), 1.0, pick)
        put = jnp.where((iota(put.shape, 1) == r) & (iota(put.shape, 0) == slot), 1.0, put)
    pick_ref[...] = pick
    put_ref[...] = put


def pick_ranges(groups, pick_ref, got_ref, out_ref, stage):
    slots = got_ref.shape[0] // groups
    stage[...] = got_ref[...].astype(f32)
    pick = pick_ref[...]
    for g in range(groups):
        value = stage[pl.ds(g, slots, stride=groups), :]
        out_ref[:, g * HEAD_DIM : (g + 1) * HEAD_DIM] = jnp.dot(
            pick, value, preferred_element_type=f32
        ).astype(bf16)


def place_before(shift):
    return (lax.axis_index("tp") // SIDE + SIDE - shift) % SIDE


def spread_queries(groups, chunks, qf, base):
    ranges = chunks[0].shape[0]
    for k, chunk in zip((0,) + SHIFTS, chunks):
        x = (lax.axis_index("tp") + SIDE - k) % SIDE
        at = pl.multiple_of(x * (groups * ranges) + base, groups * ranges)
        for g in range(groups):
            cols = slice(g * HEAD_DIM, (g + 1) * HEAD_DIM)
            qf[pl.ds(at + g * ranges, ranges), :] = chunk[:, cols].astype(f32)


def attend_row(groups, ranges, plan, k_ref, v_ref, wait_k, wait_v, out_ref, qf, base, of, lf):
    rows = SIDE * groups
    half = rows // 2
    pages, slice_tokens, pair = k_ref.shape
    scale = 1.0 / math.sqrt(HEAD_DIM)
    exp2_scale = scale * math.log2(math.e)
    top = iota((rows, HEAD_DIM), 0) < half

    def load(ref, page, span):
        return ref[pl.ds(page, span)].reshape(span * slice_tokens, pair)

    def scores(span, r, page, low, high):
        q = qf[pl.ds(base + r, rows, stride=ranges), :]
        zero = jnp.zeros_like(q)
        wide = jnp.concatenate(
            [jnp.where(top, q, zero), jnp.where(top, zero, q)], axis=1
        ).astype(bf16)
        k = load(k_ref, page, span)
        s = lax.dot_general(wide, k, (((1,), (1,)), ((), ())), preferred_element_type=f32)
        at = iota((1, span * slice_tokens), 1) + page * slice_tokens
        return s + jnp.where((at >= low) & (at < high), 0.0, VERY_LOW)

    def softmax(s):
        m = jnp.maximum(jnp.max(s, axis=1, keepdims=True), FLOOR)
        p = jnp.exp2((s - m) * exp2_scale)
        total = jnp.sum(p, axis=1, keepdims=True)
        some = total > 0.0
        safe = jnp.where(some, total, 1.0)
        lse = jnp.where(some, m * scale + jnp.log(safe), VERY_LOW)
        return p.astype(bf16), 1.0 / safe, jnp.broadcast_to(lse, (rows, HEAD_DIM))

    def values(span, page, p, inverse):
        o = jnp.dot(p, load(v_ref, page, span), preferred_element_type=f32)
        return jnp.where(top, o[:, :HEAD_DIM], o[:, HEAD_DIM:]) * inverse

    def place(r):
        return pl.ds(pl.multiple_of(r * rows, 8), rows)

    def later(e):
        return plan[RANGE_ROW, e], plan[PAGE_ROW, e], plan[LOW_ROW, e], plan[HIGH_ROW, e]

    def join(r, o, lse):
        at = place(r)
        old = lf[at, :]
        high = jnp.maximum(old, lse)
        share_old = jnp.exp(old - high)
        share = jnp.exp(lse - high)
        total = share_old + share
        of[at, :] = (of[at, :] * share_old + o * share) / total
        lf[at, :] = high + jnp.log(total)

    work = []
    for r in range(ranges):
        start = plan[START_ROW, r]
        page = jnp.minimum(start, pages - FIRST)
        work.append((FIRST, r, page, start * slice_tokens, plan[END_ROW, r]))
    for e in range(MORE):
        work.append((CHUNK, *later(e)))
    wait_k()
    parts = [scores(*w) for w in work]
    parts = [softmax(one) for one in parts]
    wait_v()
    outs = [values(w[0], w[2], p[0], p[1]) for p, w in zip(parts, work)]

    for w, (_, _, lse), o in zip(work[:ranges], parts, outs):
        of[place(w[1]), :] = o
        lf[place(w[1]), :] = lse
    for w, (_, _, lse), o in zip(work[ranges:], parts[ranges:], outs[ranges:]):
        join(w[1], o, lse)

    def few(b, carry):
        work = [later(MORE + b * FEW + j) for j in range(FEW)]
        parts = [softmax(scores(CHUNK, *w)) for w in work]
        outs = [values(CHUNK, w[1], p[0], p[1]) for p, w in zip(parts, work)]
        for w, (_, _, lse), o in zip(work, parts, outs):
            join(w[0], o, lse)
        return carry

    lax.fori_loop(0, (jnp.maximum(plan[COUNT_ROW, 0] - MORE, 0) + FEW - 1) // FEW, few, 0)

    lanes = iota((ranges, HEAD_DIM), 1)
    for x in range(SIDE):
        lse = jnp.zeros((ranges, HEAD_DIM), f32)
        for g in range(groups):
            at = pl.ds(x * groups + g, ranges, stride=rows)
            out_ref[x, :, g * HEAD_DIM : (g + 1) * HEAD_DIM] = of[at, :].astype(bf16)
            mine = (lanes == g) | (lanes == g + groups) | (lanes == g + 2 * groups)
            lse = jnp.where(mine, lf[at, :], lse)
        out_ref[x, :, groups * HEAD_DIM :] = split3(lse, lanes, groups)


def cache_copies(cache, target, shift, sems, first):
    pair = target.shape[-1]
    y = place_before(shift)
    columns = pl.ds(pl.multiple_of(y * pair, pair), pair)
    return [
        pltpu.make_async_copy(cache.at[:, w, :, columns], target.at[w], sems.at[first + w])
        for w in range(2)
    ]


def row_copy(row, held, shift, sem):
    y = place_before(shift)
    return pltpu.make_async_copy(row, held.at[pl.ds(y * SIDE, SIDE)], sem)


def attend_own(groups, plan_hbm, block, cache, held, plan, chunks, kv, row, qf, of, lf, sems):
    rows = cache_copies(cache, kv, 0, sems, 0)
    small = [pltpu.make_async_copy(plan_hbm, plan, sems.at[2])]
    small.append(pltpu.make_async_copy(block, chunks, sems.at[3]))
    for copy in small + rows:
        copy.start()
    for copy in small:
        copy.wait()
    spread_queries(groups, [chunks.at[i] for i in range(SIDE)], qf, 0)
    attend_row(
        groups, block.shape[1], plan, kv.at[0], kv.at[1], rows[0].wait, rows[1].wait, row, qf, 0, of, lf
    )
    out = row_copy(row, held, 0, sems.at[4])
    out.start()
    out.wait()


def attend_others(groups, shifts, plan_hbm, *refs):
    count = len(shifts)
    given = refs[:count]
    cache, held_in, held, plan, blocks, kv, row, qf, of, lf, sems = refs[count:]
    ranges = given[0].shape[1]
    size = SIDE * groups * ranges
    small = [pltpu.make_async_copy(plan_hbm, plan, sems.at[0])]
    for i, block in enumerate(given):
        small.append(pltpu.make_async_copy(block, blocks.at[i], sems.at[1 + i]))
    rows = [
        cache_copies(cache, kv.at[i], k, sems, 1 + count + 2 * i) for i, k in enumerate(shifts)
    ]
    for copy in small + rows[0]:
        copy.start()
    for copy in small:
        copy.wait()
    for i in range(count):
        spread_queries(groups, [blocks.at[i, j] for j in range(SIDE)], qf, i * size)
    out = 1 + 3 * count

    def one(i, carry):
        def wait(w):
            for k in range(count):

                @pl.when(i == k)
                def _():
                    rows[k][w].wait()
                    if w == 0 and k + 1 < count:
                        for copy in rows[k + 1]:
                            copy.start()

        wait_k, wait_v = functools.partial(wait, 0), functools.partial(wait, 1)
        keys, values = kv.at[i, 0], kv.at[i, 1]
        base = pl.multiple_of(i * size, size)
        attend_row(groups, ranges, plan, keys, values, wait_k, wait_v, row.at[i], qf, base, of, lf)
        shift = jnp.where(i == 0, shifts[0], shifts[-1])
        row_copy(row.at[i], held, shift, sems.at[out + i]).start()
        return carry

    lax.fori_loop(0, count, one, 0)
    for i, shift in enumerate(shifts):
        row_copy(row.at[i], held, shift, sems.at[out + i]).wait()


def merge_sources(groups, put_ref, in_ref, out_ref, stage):
    sources, ranges = in_ref.shape[0], in_ref.shape[1]
    slots = out_ref.shape[0] // PAD
    lane = iota((ranges, HEAD_DIM), 1)
    lses = [join3(in_ref[i, :, groups * HEAD_DIM :], groups) for i in range(sources)]
    top = functools.reduce(jnp.maximum, lses)
    shares = [jnp.exp(l - top) for l in lses]
    total = functools.reduce(jnp.add, shares)
    lse = top + jnp.log(total)
    inverse = 1.0 / total
    shares = [s * inverse for s in shares]
    put = put_ref[...].astype(bf16)
    for g in range(groups):
        cols = slice(g * HEAD_DIM, (g + 1) * HEAD_DIM)
        acc = jnp.zeros((ranges, HEAD_DIM), f32)
        for i in range(sources):
            acc = acc + shares[i][:, g : g + 1] * in_ref[i, :, cols].astype(f32)
        stage[pl.ds(g, slots, stride=PAD), :] = jnp.dot(
            put, acc.astype(bf16), preferred_element_type=f32
        )
    second, third = pltpu.roll(lse, groups, 1), pltpu.roll(lse, 2 * groups, 1)
    stats = jnp.where(lane < groups, lse, jnp.where(lane < 2 * groups, second, third))
    parts = split3(stats, lane, groups)
    stage[pl.ds(groups, slots, stride=PAD), :] = jnp.dot(put, parts, preferred_element_type=f32)
    for g in range(groups + 1, PAD):
        stage[pl.ds(g, slots, stride=PAD), :] = jnp.zeros((slots, HEAD_DIM), f32)
    out_ref[...] = stage[...].astype(bf16)


def finish(steps, heads, in_ref, owner_ref, q_ref, k_ref, v_ref, out_ref, stage):
    groups = steps * heads
    lenders = in_ref.shape[0] // (CAP * PAD)
    scale = 1.0 / math.sqrt(HEAD_DIM)
    stage[...] = in_ref[...].astype(f32)

    def group(g):
        return jnp.concatenate(
            [stage[pl.ds(c * PAD + g, lenders, stride=CAP * PAD), :] for c in range(CAP)], axis=0
        )

    lses = jnp.transpose(join3(group(groups), groups), (1, 0))
    owned = owner_ref[...].astype(jnp.int32) == iota(owner_ref.shape, 0)
    keys = [k_ref[t].astype(f32) for t in range(steps)]
    values = [v_ref[t].astype(f32) for t in range(steps)]
    for s in range(steps):
        for h in range(heads):
            g = s * heads + h
            cols = slice(h * HEAD_DIM, (h + 1) * HEAD_DIM)
            q = q_ref[s, :, cols].astype(f32)
            scores = [
                jnp.sum(q * keys[t], axis=1, keepdims=True) * scale for t in range(s + 1)
            ]
            lent = jnp.where(owned, jnp.broadcast_to(lses[g : g + 1, :], owned.shape), VERY_LOW)
            top = functools.reduce(jnp.maximum, scores)
            top = jnp.maximum(top, jnp.max(lent, axis=1, keepdims=True))
            share = jnp.where(owned, jnp.exp(lent - top), 0.0)
            total = jnp.sum(share, axis=1, keepdims=True)
            high = share.astype(bf16).astype(f32)
            parts = jnp.concatenate([high, share - high], axis=0).astype(bf16)
            sums = jnp.dot(parts, group(g).astype(bf16), preferred_element_type=f32)
            acc = sums[: len(share)] + sums[len(share) :]
            for t in range(s + 1):
                weight = jnp.exp(scores[t] - top)
                total = total + weight
                acc = acc + weight.astype(bf16).astype(f32) * values[t]
            out_ref[s, :, cols] = (acc / total).astype(bf16)


def x_shift(k):
    return [(SIDE * y + x, SIDE * y + (x + k) % SIDE) for y in range(SIDE) for x in range(SIDE)]


def y_shift(k):
    return [(SIDE * y + x, SIDE * ((y + k) % SIDE) + x) for y in range(SIDE) for x in range(SIDE)]


def on_device(queries, new_kv, page_cache, range_owner, range_start, range_tokens):
    steps, requests, columns = queries.shape
    lenders = lax.axis_size("inst")
    tp_count = lax.axis_size("tp")
    my_tp = lax.axis_index("tp")
    pages, _, slice_tokens, kv_columns = page_cache.shape
    ranges = range_owner.shape[1]
    heads = columns // HEAD_DIM
    groups = steps * heads
    kv_heads = kv_columns // HEAD_DIM
    group_size = heads * tp_count // kv_heads
    slots = lenders * CAP
    wide = (groups + 1) * HEAD_DIM
    vmem = pl.BlockSpec(memory_space=pltpu.VMEM)
    smem = pl.BlockSpec(memory_space=pltpu.SMEM)
    hbm = pl.BlockSpec(memory_space=pltpu.HBM)
    params = pltpu.CompilerParams(vmem_limit_bytes=24 * 2**20)
    grant = pltpu.CompilerParams(vmem_limit_bytes=57 * 2**20)
    whole = pltpu.CompilerParams(vmem_limit_bytes=64 * 2**20 - 2**17)
    dma = pltpu.SemaphoreType.DMA

    sent, slot_owner = pl.pallas_call(
        prepare,
        in_specs=[hbm] * 2,
        out_specs=[vmem] * 2,
        out_shape=[
            jax.ShapeDtypeStruct((slots * groups, HEAD_DIM), bf16),
            jax.ShapeDtypeStruct((requests, slots), f32),
        ],
        scratch_shapes=[
            pltpu.VMEM(queries.shape, bf16),
            pltpu.VMEM(range_owner.shape, jnp.int32),
            pltpu.VMEM((slots * groups, HEAD_DIM), f32),
            dma((2,)),
        ],
        compiler_params=whole,
        name="prepare",
    )(queries, range_owner)
    got = lax.all_to_all(sent, "inst", split_axis=0, concat_axis=0, tiled=True)

    plan, pick, put = pl.pallas_call(
        functools.partial(make_plan, slice_tokens, pages),
        in_specs=[smem] * 3,
        out_specs=[smem, vmem, vmem],
        out_shape=[
            jax.ShapeDtypeStruct((8, ranges), jnp.int32),
            jax.ShapeDtypeStruct((ranges, slots), f32),
            jax.ShapeDtypeStruct((slots, ranges), f32),
        ],
        compiler_params=params,
        name="make_plan",
    )(range_owner, range_start, range_tokens)
    head = my_tp * heads // group_size
    fresh = lax.dynamic_slice_in_dim(new_kv, head * HEAD_DIM, HEAD_DIM, axis=3)

    own = pl.pallas_call(
        functools.partial(pick_ranges, groups),
        in_specs=[vmem] * 2,
        out_specs=vmem,
        out_shape=jax.ShapeDtypeStruct((ranges, groups * HEAD_DIM), bf16),
        scratch_shapes=[pltpu.VMEM((slots * groups, HEAD_DIM), f32)],
        compiler_params=params,
        name="pick_ranges",
    )(pick, got)
    block = jnp.stack([own] + [lax.ppermute(own, "tp", x_shift(k)) for k in SHIFTS])
    near = {k: lax.ppermute(block, "tp", y_shift(k)) for k in (1, SIDE - 1)}

    pair = 2 * HEAD_DIM
    size = SIDE * groups * ranges
    partial_type = jax.ShapeDtypeStruct((tp_count, ranges, wide), bf16)
    plan_type = pltpu.SMEM(plan.shape, jnp.int32)
    row_scratch = [pltpu.VMEM((size, HEAD_DIM), f32)] * 2
    partial = pl.pallas_call(
        functools.partial(attend_own, groups),
        in_specs=[hbm] * 3,
        out_specs=hbm,
        out_shape=partial_type,
        scratch_shapes=[
            plan_type,
            pltpu.VMEM((SIDE, ranges, groups * HEAD_DIM), bf16),
            pltpu.VMEM((2, pages, slice_tokens, pair), bf16),
            pltpu.VMEM((SIDE, ranges, wide), bf16),
            pltpu.VMEM((size + ranges, HEAD_DIM), f32),
        ]
        + row_scratch
        + [dma((5,))],
        compiler_params=grant,
        cost_estimate=pl.CostEstimate(flops=10**9, bytes_accessed=2**23, transcendentals=0),
        name="attend_own",
    )(plan, block, page_cache)
    passed, partial = lax.optimization_barrier((near[1], partial))
    far = lax.ppermute(passed, "tp", y_shift(1))
    for given in ({1: passed, SIDE - 1: near[SIDE - 1]}, {2: far}):
        count = len(given)
        partial = pl.pallas_call(
            functools.partial(attend_others, groups, list(given)),
            in_specs=[hbm] * (count + 3),
            out_specs=hbm,
            out_shape=partial_type,
            scratch_shapes=[
                plan_type,
                pltpu.VMEM((count, SIDE, ranges, groups * HEAD_DIM), bf16),
                pltpu.VMEM((count, 2, pages, slice_tokens, pair), bf16),
                pltpu.VMEM((count, SIDE, ranges, wide), bf16),
                pltpu.VMEM((count * size + ranges, HEAD_DIM), f32),
            ]
            + row_scratch
            + [dma((1 + 4 * count,))],
            input_output_aliases={count + 2: 0},
            compiler_params=whole,
            cost_estimate=pl.CostEstimate(
                flops=count * 10**9, bytes_accessed=count * 2**22, transcendentals=0
            ),
            name="attend_others",
        )(plan, *given.values(), page_cache, partial)

    parts = lax.all_to_all(partial, "tp", split_axis=0, concat_axis=0, tiled=True)
    lent = pl.pallas_call(
        functools.partial(merge_sources, groups),
        in_specs=[vmem] * 2,
        out_specs=vmem,
        out_shape=jax.ShapeDtypeStruct((slots * PAD, HEAD_DIM), bf16),
        scratch_shapes=[pltpu.VMEM((slots * PAD, HEAD_DIM), f32)],
        compiler_params=params,
        name="merge_sources",
    )(put, parts)
    back = lax.all_to_all(lent, "inst", split_axis=0, concat_axis=0, tiled=True)
    return pl.pallas_call(
        functools.partial(finish, steps, heads),
        in_specs=[vmem] * 5,
        out_specs=vmem,
        out_shape=jax.ShapeDtypeStruct((steps, requests, columns), bf16),
        scratch_shapes=[pltpu.VMEM((slots * PAD, HEAD_DIM), f32)],
        compiler_params=params,
        name="finish",
    )(back, slot_owner, queries, fresh[:, :, 0], fresh[:, :, 1])


def solution(mesh):
    placed = (
        P(None, "inst", "tp"),
        P(None, "inst", None, None),
        P("inst", None, "tp", None),
        P(),
        P(),
        P(),
    )
    return jax.shard_map(
        on_device, mesh=mesh, in_specs=placed, out_specs=P(None, "inst", "tp"), check_vma=False
    )
```

```python
import functools
import math

import jax
import jax.numpy as jnp
from jax import lax
from jax.experimental import pallas as pl
from jax.experimental.pallas import tpu as pltpu
from jax.sharding import PartitionSpec as P

HEAD_DIM = 128
PAGE = 256
CAP = 2
REQ_INST = 8
SIDE = 4
SHIFTS = (1, 3, 2)
FIRST = 8
CHUNK = 16
MORE = 8
FEW = 2
VERY_LOW = -1e30
FLOOR = -1e29
PAD = 16
PAGE_ROW, LOW_ROW, HIGH_ROW, RANGE_ROW, END_ROW, COUNT_ROW, START_ROW = range(7)

f32 = jnp.float32
bf16 = jnp.bfloat16


def iota(shape, dim):
    return lax.broadcasted_iota(jnp.int32, shape, dim)


def split3(stats, lane, groups):
    high = stats.astype(bf16).astype(f32)
    rest = stats - high
    mid = rest.astype(bf16).astype(f32)
    low = rest - mid
    return jnp.where(lane < groups, high, jnp.where(lane < 2 * groups, mid, low)).astype(bf16)


def join3(parts, groups):
    parts = parts.astype(f32)
    return (
        parts
        + pltpu.roll(parts, HEAD_DIM - groups, 1)
        + pltpu.roll(parts, HEAD_DIM - 2 * groups, 1)
    )


def slot_owners(owner):
    lenders, ranges = owner.shape
    hit = owner // REQ_INST == lax.axis_index("inst")
    earlier = (iota((ranges, ranges), 0) < iota((ranges, ranges), 1)).astype(f32)
    rank = jnp.dot(hit.astype(f32), earlier, preferred_element_type=f32)
    local = (owner % REQ_INST + 1).astype(f32)
    owners = []
    for c in range(CAP):
        chosen = jnp.where(hit & (jnp.abs(rank - c) < 0.5), local, 0.0)
        owners.append(jnp.sum(chosen, axis=1, keepdims=True) - 1.0)
    return owners


def prepare(q_hbm, owner_hbm, sent_ref, q_ref, owner_ref, stage, sems):
    copies = [
        pltpu.make_async_copy(owner_hbm, owner_ref, sems.at[0]),
        pltpu.make_async_copy(q_hbm, q_ref, sems.at[1]),
    ]
    for copy in copies:
        copy.start()
    steps, requests, columns = q_ref.shape
    heads = columns // HEAD_DIM
    groups = steps * heads
    lenders, ranges = owner_ref.shape
    copies[0].wait()
    owners = slot_owners(owner_ref[...])
    copies[1].wait()
    for c in range(CAP):
        pick = (owners[c].astype(jnp.int32) == iota((lenders, requests), 1)).astype(f32)
        for s in range(steps):
            value = jnp.dot(pick, q_ref[s].astype(f32), preferred_element_type=f32)
            for h in range(heads):
                at = pl.ds(c * groups + s * heads + h, lenders, stride=CAP * groups)
                stage[at, :] = value[:, h * HEAD_DIM : (h + 1) * HEAD_DIM]
    sent_ref[...] = stage[...].astype(bf16)


def make_plan(slice_tokens, pages, owner_ref, start_ref, tokens_ref, plan, pick_ref, put_ref):
    ranges = owner_ref.shape[1]
    me = lax.axis_index("inst")
    my_tp = lax.axis_index("tp")
    for i in range(RANGE_ROW + 1):
        for r in range(ranges):
            plan[i, r] = 0

    def fill(r, count):
        start = start_ref[me, r]
        tokens = tokens_ref[me, r]
        span = (tokens + PAGE - 1) // PAGE
        more = jnp.maximum(span - FIRST + CHUNK - 1, 0) // CHUNK
        tail = jnp.clip(tokens % PAGE - my_tp * slice_tokens, 0, slice_tokens)
        high = (start + tokens // PAGE) * slice_tokens + tail
        plan[END_ROW, r] = high
        plan[START_ROW, r] = start

        def one(j, carry):
            first = start + FIRST + j * CHUNK
            plan[PAGE_ROW, count + j] = jnp.minimum(first, pages - CHUNK)
            plan[LOW_ROW, count + j] = first * slice_tokens
            plan[HIGH_ROW, count + j] = high
            plan[RANGE_ROW, count + j] = r
            return carry

        lax.fori_loop(0, more, one, 0)
        return count + more

    plan[COUNT_ROW, 0] = lax.fori_loop(0, ranges, fill, 0)
    homes = [owner_ref[me, r] // REQ_INST for r in range(ranges)]
    pick = jnp.zeros(pick_ref.shape, f32)
    put = jnp.zeros(put_ref.shape, f32)
    for r in range(ranges):
        rank = sum([(homes[e] == homes[r]).astype(jnp.int32) for e in range(r)], jnp.int32(0))
        slot = homes[r] * CAP + rank
        pick = jnp.where((iota(pick.shape, 0) == r) & (iota(pick.shape, 1) == slot), 1.0, pick)
        put = jnp.where((iota(put.shape, 1) == r) & (iota(put.shape, 0) == slot), 1.0, put)
    pick_ref[...] = pick
    put_ref[...] = put


def pick_ranges(groups, pick_ref, got_ref, out_ref, stage):
    slots = got_ref.shape[0] // groups
    stage[...] = got_ref[...].astype(f32)
    pick = pick_ref[...]
    for g in range(groups):
        value = stage[pl.ds(g, slots, stride=groups), :]
        out_ref[:, g * HEAD_DIM : (g + 1) * HEAD_DIM] = jnp.dot(
            pick, value, preferred_element_type=f32
        ).astype(bf16)


def place_before(shift):
    return (lax.axis_index("tp") // SIDE + SIDE - shift) % SIDE


def spread_queries(groups, chunks, qf, base):
    ranges = chunks[0].shape[0]
    for k, chunk in zip((0,) + SHIFTS, chunks):
        x = (lax.axis_index("tp") + SIDE - k) % SIDE
        at = pl.multiple_of(x * (groups * ranges) + base, groups * ranges)
        for g in range(groups):
            cols = slice(g * HEAD_DIM, (g + 1) * HEAD_DIM)
            qf[pl.ds(at + g * ranges, ranges), :] = chunk[:, cols].astype(f32)


def attend_row(groups, ranges, plan, k_ref, v_ref, wait_k, wait_v, out_ref, qf, base, of, lf):
    rows = SIDE * groups
    half = rows // 2
    pages, slice_tokens, pair = k_ref.shape
    scale = 1.0 / math.sqrt(HEAD_DIM)
    exp2_scale = scale * math.log2(math.e)
    top = iota((rows, HEAD_DIM), 0) < half

    def load(ref, page, span):
        return ref[pl.ds(page, span)].reshape(span * slice_tokens, pair)

    def scores(span, r, page, low, high):
        q = qf[pl.ds(base + r, rows, stride=ranges), :]
        zero = jnp.zeros_like(q)
        wide = jnp.concatenate(
            [jnp.where(top, q, zero), jnp.where(top, zero, q)], axis=1
        ).astype(bf16)
        k = load(k_ref, page, span)
        s = lax.dot_general(wide, k, (((1,), (1,)), ((), ())), preferred_element_type=f32)
        at = iota((1, span * slice_tokens), 1) + page * slice_tokens
        return s + jnp.where((at >= low) & (at < high), 0.0, VERY_LOW)

    def softmax(s):
        m = jnp.maximum(jnp.max(s, axis=1, keepdims=True), FLOOR)
        p = jnp.exp2((s - m) * exp2_scale)
        total = jnp.sum(p, axis=1, keepdims=True)
        some = total > 0.0
        safe = jnp.where(some, total, 1.0)
        lse = jnp.where(some, m * scale + jnp.log(safe), VERY_LOW)
        return p.astype(bf16), 1.0 / safe, jnp.broadcast_to(lse, (rows, HEAD_DIM))

    def values(span, page, p, inverse):
        o = jnp.dot(p, load(v_ref, page, span), preferred_element_type=f32)
        return jnp.where(top, o[:, :HEAD_DIM], o[:, HEAD_DIM:]) * inverse

    def place(r):
        return pl.ds(pl.multiple_of(r * rows, 8), rows)

    def later(e):
        return plan[RANGE_ROW, e], plan[PAGE_ROW, e], plan[LOW_ROW, e], plan[HIGH_ROW, e]

    def join(r, o, lse):
        at = place(r)
        old = lf[at, :]
        high = jnp.maximum(old, lse)
        share_old = jnp.exp(old - high)
        share = jnp.exp(lse - high)
        total = share_old + share
        of[at, :] = (of[at, :] * share_old + o * share) / total
        lf[at, :] = high + jnp.log(total)

    work = []
    for r in range(ranges):
        start = plan[START_ROW, r]
        page = jnp.minimum(start, pages - FIRST)
        work.append((FIRST, r, page, start * slice_tokens, plan[END_ROW, r]))
    for e in range(MORE):
        work.append((CHUNK, *later(e)))
    wait_k()
    parts = [scores(*w) for w in work]
    parts = [softmax(one) for one in parts]
    wait_v()
    outs = [values(w[0], w[2], p[0], p[1]) for p, w in zip(parts, work)]

    for w, (_, _, lse), o in zip(work[:ranges], parts, outs):
        of[place(w[1]), :] = o
        lf[place(w[1]), :] = lse
    for w, (_, _, lse), o in zip(work[ranges:], parts[ranges:], outs[ranges:]):
        join(w[1], o, lse)

    def few(b, carry):
        work = [later(MORE + b * FEW + j) for j in range(FEW)]
        parts = [softmax(scores(CHUNK, *w)) for w in work]
        outs = [values(CHUNK, w[1], p[0], p[1]) for p, w in zip(parts, work)]
        for w, (_, _, lse), o in zip(work, parts, outs):
            join(w[0], o, lse)
        return carry

    lax.fori_loop(0, (jnp.maximum(plan[COUNT_ROW, 0] - MORE, 0) + FEW - 1) // FEW, few, 0)

    lanes = iota((ranges, HEAD_DIM), 1)
    for x in range(SIDE):
        lse = jnp.zeros((ranges, HEAD_DIM), f32)
        for g in range(groups):
            at = pl.ds(x * groups + g, ranges, stride=rows)
            out_ref[x, :, g * HEAD_DIM : (g + 1) * HEAD_DIM] = of[at, :].astype(bf16)
            mine = (lanes == g) | (lanes == g + groups) | (lanes == g + 2 * groups)
            lse = jnp.where(mine, lf[at, :], lse)
        out_ref[x, :, groups * HEAD_DIM :] = split3(lse, lanes, groups)


def cache_copies(cache, target, shift, sems, first):
    pair = target.shape[-1]
    y = place_before(shift)
    columns = pl.ds(pl.multiple_of(y * pair, pair), pair)
    return [
        pltpu.make_async_copy(cache.at[:, w, :, columns], target.at[w], sems.at[first + w])
        for w in range(2)
    ]


def row_copy(row, held, shift, sem):
    y = place_before(shift)
    return pltpu.make_async_copy(row, held.at[pl.ds(y * SIDE, SIDE)], sem)


def attend_own(groups, plan_hbm, block, cache, held, plan, chunks, kv, row, qf, of, lf, sems):
    rows = cache_copies(cache, kv, 0, sems, 0)
    small = [pltpu.make_async_copy(plan_hbm, plan, sems.at[2])]
    small.append(pltpu.make_async_copy(block, chunks, sems.at[3]))
    for copy in small + rows:
        copy.start()
    for copy in small:
        copy.wait()
    spread_queries(groups, [chunks.at[i] for i in range(SIDE)], qf, 0)
    attend_row(
        groups, block.shape[1], plan, kv.at[0], kv.at[1], rows[0].wait, rows[1].wait, row, qf, 0, of, lf
    )
    out = row_copy(row, held, 0, sems.at[4])
    out.start()
    out.wait()


def attend_others(groups, shifts, plan_hbm, *refs):
    count = len(shifts)
    given = refs[:count]
    cache, held_in, held, plan, blocks, kv, row, qf, of, lf, sems = refs[count:]
    ranges = given[0].shape[1]
    size = SIDE * groups * ranges
    small = [pltpu.make_async_copy(plan_hbm, plan, sems.at[0])]
    for i, block in enumerate(given):
        small.append(pltpu.make_async_copy(block, blocks.at[i], sems.at[1 + i]))
    rows = [
        cache_copies(cache, kv.at[i], k, sems, 1 + count + 2 * i) for i, k in enumerate(shifts)
    ]
    for copy in small + rows[0]:
        copy.start()
    for copy in small:
        copy.wait()
    for i in range(count):
        spread_queries(groups, [blocks.at[i, j] for j in range(SIDE)], qf, i * size)
    out = 1 + 3 * count

    def one(i, carry):
        def wait(w):
            for k in range(count):

                @pl.when(i == k)
                def _():
                    rows[k][w].wait()
                    if w == 0 and k + 1 < count:
                        for copy in rows[k + 1]:
                            copy.start()

        wait_k, wait_v = functools.partial(wait, 0), functools.partial(wait, 1)
        keys, values = kv.at[i, 0], kv.at[i, 1]
        base = pl.multiple_of(i * size, size)
        attend_row(groups, ranges, plan, keys, values, wait_k, wait_v, row.at[i], qf, base, of, lf)
        shift = jnp.where(i == 0, shifts[0], shifts[-1])
        row_copy(row.at[i], held, shift, sems.at[out + i]).start()
        return carry

    lax.fori_loop(0, count, one, 0)
    for i, shift in enumerate(shifts):
        row_copy(row.at[i], held, shift, sems.at[out + i]).wait()


def merge_sources(groups, put_ref, in_ref, out_ref, stage):
    sources, ranges = in_ref.shape[0], in_ref.shape[1]
    slots = out_ref.shape[0] // PAD
    lane = iota((ranges, HEAD_DIM), 1)
    lses = [join3(in_ref[i, :, groups * HEAD_DIM :], groups) for i in range(sources)]
    top = functools.reduce(jnp.maximum, lses)
    shares = [jnp.exp(l - top) for l in lses]
    total = functools.reduce(jnp.add, shares)
    lse = top + jnp.log(total)
    inverse = 1.0 / total
    shares = [s * inverse for s in shares]
    put = put_ref[...].astype(bf16)
    for g in range(groups):
        cols = slice(g * HEAD_DIM, (g + 1) * HEAD_DIM)
        acc = jnp.zeros((ranges, HEAD_DIM), f32)
        for i in range(sources):
            acc = acc + shares[i][:, g : g + 1] * in_ref[i, :, cols].astype(f32)
        stage[pl.ds(g, slots, stride=PAD), :] = jnp.dot(
            put, acc.astype(bf16), preferred_element_type=f32
        )
    second, third = pltpu.roll(lse, groups, 1), pltpu.roll(lse, 2 * groups, 1)
    stats = jnp.where(lane < groups, lse, jnp.where(lane < 2 * groups, second, third))
    parts = split3(stats, lane, groups)
    stage[pl.ds(groups, slots, stride=PAD), :] = jnp.dot(put, parts, preferred_element_type=f32)
    for g in range(groups + 1, PAD):
        stage[pl.ds(g, slots, stride=PAD), :] = jnp.zeros((slots, HEAD_DIM), f32)
    out_ref[...] = stage[...].astype(bf16)


def slot_table(owner_ref, mine_ref):
    lenders = owner_ref.shape[0]
    spread = [jnp.broadcast_to(mine, (lenders, HEAD_DIM)) for mine in slot_owners(owner_ref[...])]
    mine_ref[...] = jnp.transpose(jnp.concatenate(spread, axis=0), (1, 0))[: mine_ref.shape[0], :]


def finish(steps, heads, in_ref, owner_ref, q_ref, k_ref, v_ref, out_ref, stage):
    groups = steps * heads
    lenders = in_ref.shape[0] // (CAP * PAD)
    scale = 1.0 / math.sqrt(HEAD_DIM)
    stage[...] = in_ref[...].astype(f32)

    def group(g):
        return jnp.concatenate(
            [stage[pl.ds(c * PAD + g, lenders, stride=CAP * PAD), :] for c in range(CAP)], axis=0
        )

    lses = jnp.transpose(join3(group(groups), groups), (1, 0))
    owned = owner_ref[...].astype(jnp.int32) == iota(owner_ref.shape, 0)
    keys = [k_ref[t].astype(f32) for t in range(steps)]
    values = [v_ref[t].astype(f32) for t in range(steps)]
    for s in range(steps):
        for h in range(heads):
            g = s * heads + h
            cols = slice(h * HEAD_DIM, (h + 1) * HEAD_DIM)
            q = q_ref[s, :, cols].astype(f32)
            scores = [
                jnp.sum(q * keys[t], axis=1, keepdims=True) * scale for t in range(s + 1)
            ]
            lent = jnp.where(owned, jnp.broadcast_to(lses[g : g + 1, :], owned.shape), VERY_LOW)
            top = functools.reduce(jnp.maximum, scores)
            top = jnp.maximum(top, jnp.max(lent, axis=1, keepdims=True))
            share = jnp.where(owned, jnp.exp(lent - top), 0.0)
            total = jnp.sum(share, axis=1, keepdims=True)
            high = share.astype(bf16).astype(f32)
            parts = jnp.concatenate([high, share - high], axis=0).astype(bf16)
            sums = jnp.dot(parts, group(g).astype(bf16), preferred_element_type=f32)
            acc = sums[: len(share)] + sums[len(share) :]
            for t in range(s + 1):
                weight = jnp.exp(scores[t] - top)
                total = total + weight
                acc = acc + weight.astype(bf16).astype(f32) * values[t]
            out_ref[s, :, cols] = (acc / total).astype(bf16)


def x_shift(k):
    return [(SIDE * y + x, SIDE * y + (x + k) % SIDE) for y in range(SIDE) for x in range(SIDE)]


def y_shift(k):
    return [(SIDE * y + x, SIDE * ((y + k) % SIDE) + x) for y in range(SIDE) for x in range(SIDE)]


def on_device(queries, new_kv, page_cache, range_owner, range_start, range_tokens):
    steps, requests, columns = queries.shape
    lenders = lax.axis_size("inst")
    tp_count = lax.axis_size("tp")
    my_tp = lax.axis_index("tp")
    pages, _, slice_tokens, kv_columns = page_cache.shape
    ranges = range_owner.shape[1]
    heads = columns // HEAD_DIM
    groups = steps * heads
    kv_heads = kv_columns // HEAD_DIM
    group_size = heads * tp_count // kv_heads
    slots = lenders * CAP
    wide = (groups + 1) * HEAD_DIM
    vmem = pl.BlockSpec(memory_space=pltpu.VMEM)
    smem = pl.BlockSpec(memory_space=pltpu.SMEM)
    hbm = pl.BlockSpec(memory_space=pltpu.HBM)
    params = pltpu.CompilerParams(vmem_limit_bytes=24 * 2**20)
    grant = pltpu.CompilerParams(vmem_limit_bytes=57 * 2**20)
    whole = pltpu.CompilerParams(vmem_limit_bytes=64 * 2**20 - 2**17)
    dma = pltpu.SemaphoreType.DMA

    sent = pl.pallas_call(
        prepare,
        in_specs=[hbm] * 2,
        out_specs=vmem,
        out_shape=jax.ShapeDtypeStruct((slots * groups, HEAD_DIM), bf16),
        scratch_shapes=[
            pltpu.VMEM(queries.shape, bf16),
            pltpu.VMEM(range_owner.shape, jnp.int32),
            pltpu.VMEM((slots * groups, HEAD_DIM), f32),
            dma((2,)),
        ],
        compiler_params=whole,
        name="prepare",
    )(queries, range_owner)
    got = lax.all_to_all(sent, "inst", split_axis=0, concat_axis=0, tiled=True)

    plan, pick, put = pl.pallas_call(
        functools.partial(make_plan, slice_tokens, pages),
        in_specs=[smem] * 3,
        out_specs=[smem, vmem, vmem],
        out_shape=[
            jax.ShapeDtypeStruct((8, ranges), jnp.int32),
            jax.ShapeDtypeStruct((ranges, slots), f32),
            jax.ShapeDtypeStruct((slots, ranges), f32),
        ],
        compiler_params=params,
        name="make_plan",
    )(range_owner, range_start, range_tokens)
    own = pl.pallas_call(
        functools.partial(pick_ranges, groups),
        in_specs=[vmem] * 2,
        out_specs=vmem,
        out_shape=jax.ShapeDtypeStruct((ranges, groups * HEAD_DIM), bf16),
        scratch_shapes=[pltpu.VMEM((slots * groups, HEAD_DIM), f32)],
        compiler_params=params,
        name="pick_ranges",
    )(pick, got)
    block = jnp.stack([own] + [lax.ppermute(own, "tp", x_shift(k)) for k in SHIFTS])
    near = {k: lax.ppermute(block, "tp", y_shift(k)) for k in (1, SIDE - 1)}

    pair = 2 * HEAD_DIM
    size = SIDE * groups * ranges
    partial_type = jax.ShapeDtypeStruct((tp_count, ranges, wide), bf16)
    plan_type = pltpu.SMEM(plan.shape, jnp.int32)
    row_scratch = [pltpu.VMEM((size, HEAD_DIM), f32)] * 2
    partial = pl.pallas_call(
        functools.partial(attend_own, groups),
        in_specs=[hbm] * 3,
        out_specs=hbm,
        out_shape=partial_type,
        scratch_shapes=[
            plan_type,
            pltpu.VMEM((SIDE, ranges, groups * HEAD_DIM), bf16),
            pltpu.VMEM((2, pages, slice_tokens, pair), bf16),
            pltpu.VMEM((SIDE, ranges, wide), bf16),
            pltpu.VMEM((size + ranges, HEAD_DIM), f32),
        ]
        + row_scratch
        + [dma((5,))],
        compiler_params=grant,
        cost_estimate=pl.CostEstimate(flops=10**9, bytes_accessed=2**23, transcendentals=0),
        name="attend_own",
    )(plan, block, page_cache)
    passed, partial = lax.optimization_barrier((near[1], partial))
    far = lax.ppermute(passed, "tp", y_shift(1))
    for given in ({1: passed, SIDE - 1: near[SIDE - 1]}, {2: far}):
        count = len(given)
        partial = pl.pallas_call(
            functools.partial(attend_others, groups, list(given)),
            in_specs=[hbm] * (count + 3),
            out_specs=hbm,
            out_shape=partial_type,
            scratch_shapes=[
                plan_type,
                pltpu.VMEM((count, SIDE, ranges, groups * HEAD_DIM), bf16),
                pltpu.VMEM((count, 2, pages, slice_tokens, pair), bf16),
                pltpu.VMEM((count, SIDE, ranges, wide), bf16),
                pltpu.VMEM((count * size + ranges, HEAD_DIM), f32),
            ]
            + row_scratch
            + [dma((1 + 4 * count,))],
            input_output_aliases={count + 2: 0},
            compiler_params=whole,
            cost_estimate=pl.CostEstimate(
                flops=count * 10**9, bytes_accessed=count * 2**22, transcendentals=0
            ),
            name="attend_others",
        )(plan, *given.values(), page_cache, partial)

    parts = lax.all_to_all(partial, "tp", split_axis=0, concat_axis=0, tiled=True)
    lent = pl.pallas_call(
        functools.partial(merge_sources, groups),
        in_specs=[vmem] * 2,
        out_specs=vmem,
        out_shape=jax.ShapeDtypeStruct((slots * PAD, HEAD_DIM), bf16),
        scratch_shapes=[pltpu.VMEM((slots * PAD, HEAD_DIM), f32)],
        compiler_params=params,
        name="merge_sources",
    )(put, parts)
    back = lax.all_to_all(lent, "inst", split_axis=0, concat_axis=0, tiled=True)
    lent, new_kv, owners = lax.optimization_barrier((lent, new_kv, range_owner))
    head = my_tp * heads // group_size
    fresh = lax.dynamic_slice_in_dim(new_kv, head * HEAD_DIM, HEAD_DIM, axis=3)
    slot_owner = pl.pallas_call(
        slot_table,
        in_specs=[vmem],
        out_specs=vmem,
        out_shape=jax.ShapeDtypeStruct((requests, slots), f32),
        compiler_params=params,
        name="slot_table",
    )(owners)
    return pl.pallas_call(
        functools.partial(finish, steps, heads),
        in_specs=[vmem] * 5,
        out_specs=vmem,
        out_shape=jax.ShapeDtypeStruct((steps, requests, columns), bf16),
        scratch_shapes=[pltpu.VMEM((slots * PAD, HEAD_DIM), f32)],
        compiler_params=params,
        name="finish",
    )(back, slot_owner, queries, fresh[:, :, 0], fresh[:, :, 1])


def solution(mesh):
    placed = (
        P(None, "inst", "tp"),
        P(None, "inst", None, None),
        P("inst", None, "tp", None),
        P(),
        P(),
        P(),
    )
    return jax.shard_map(
        on_device, mesh=mesh, in_specs=placed, out_specs=P(None, "inst", "tp"), check_vma=False
    )
```

```python
import functools
import math

import jax
import jax.numpy as jnp
from jax import lax
from jax.experimental import pallas as pl
from jax.experimental.pallas import tpu as pltpu
from jax.sharding import PartitionSpec as P

HEAD_DIM = 128
PAGE = 256
CAP = 2
REQ_INST = 8
SIDE = 4
SHIFTS = (1, 3, 2)
FIRST = 8
CHUNK = 16
MORE = 8
FEW = 2
VERY_LOW = -1e30
FLOOR = -1e29
PAD = 16
PAGE_ROW, LOW_ROW, HIGH_ROW, RANGE_ROW, END_ROW, COUNT_ROW, START_ROW = range(7)

f32 = jnp.float32
bf16 = jnp.bfloat16


def iota(shape, dim):
    return lax.broadcasted_iota(jnp.int32, shape, dim)


def split3(stats, lane, groups):
    high = stats.astype(bf16).astype(f32)
    rest = stats - high
    mid = rest.astype(bf16).astype(f32)
    low = rest - mid
    return jnp.where(lane < groups, high, jnp.where(lane < 2 * groups, mid, low)).astype(bf16)


def join3(parts, groups):
    parts = parts.astype(f32)
    return (
        parts
        + pltpu.roll(parts, HEAD_DIM - groups, 1)
        + pltpu.roll(parts, HEAD_DIM - 2 * groups, 1)
    )


def prepare(q_hbm, owner_hbm, sent_ref, mine_ref, q_ref, owner_ref, stage, sems):
    copies = [
        pltpu.make_async_copy(owner_hbm, owner_ref, sems.at[0]),
        pltpu.make_async_copy(q_hbm, q_ref, sems.at[1]),
    ]
    for copy in copies:
        copy.start()
    steps, requests, columns = q_ref.shape
    heads = columns // HEAD_DIM
    groups = steps * heads
    lenders, ranges = owner_ref.shape
    earlier = (iota((ranges, ranges), 0) < iota((ranges, ranges), 1)).astype(f32)
    copies[0].wait()
    owner = owner_ref[...]
    hit = owner // REQ_INST == lax.axis_index("inst")
    rank = jnp.dot(hit.astype(f32), earlier, preferred_element_type=f32)
    local = (owner % REQ_INST + 1).astype(f32)
    owners = []
    for c in range(CAP):
        chosen = jnp.where(hit & (jnp.abs(rank - c) < 0.5), local, 0.0)
        owners.append(jnp.sum(chosen, axis=1, keepdims=True) - 1.0)
    copies[1].wait()
    for c in range(CAP):
        pick = (owners[c].astype(jnp.int32) == iota((lenders, requests), 1)).astype(f32)
        for s in range(steps):
            value = jnp.dot(pick, q_ref[s].astype(f32), preferred_element_type=f32)
            for h in range(heads):
                at = pl.ds(c * groups + s * heads + h, lenders, stride=CAP * groups)
                stage[at, :] = value[:, h * HEAD_DIM : (h + 1) * HEAD_DIM]
    sent_ref[...] = stage[...].astype(bf16)
    spread = [jnp.broadcast_to(mine, (lenders, HEAD_DIM)) for mine in owners]
    mine_ref[...] = jnp.transpose(jnp.concatenate(spread, axis=0), (1, 0))[: mine_ref.shape[0], :]


def make_plan(slice_tokens, pages, owner_ref, start_ref, tokens_ref, plan, pick_ref, put_ref):
    ranges = owner_ref.shape[1]
    me = lax.axis_index("inst")
    my_tp = lax.axis_index("tp")
    for i in range(RANGE_ROW + 1):
        for r in range(ranges):
            plan[i, r] = 0

    def fill(r, count):
        start = start_ref[me, r]
        tokens = tokens_ref[me, r]
        span = (tokens + PAGE - 1) // PAGE
        more = jnp.maximum(span - FIRST + CHUNK - 1, 0) // CHUNK
        tail = jnp.clip(tokens % PAGE - my_tp * slice_tokens, 0, slice_tokens)
        high = (start + tokens // PAGE) * slice_tokens + tail
        plan[END_ROW, r] = high
        plan[START_ROW, r] = start

        def one(j, carry):
            first = start + FIRST + j * CHUNK
            plan[PAGE_ROW, count + j] = jnp.minimum(first, pages - CHUNK)
            plan[LOW_ROW, count + j] = first * slice_tokens
            plan[HIGH_ROW, count + j] = high
            plan[RANGE_ROW, count + j] = r
            return carry

        lax.fori_loop(0, more, one, 0)
        return count + more

    plan[COUNT_ROW, 0] = lax.fori_loop(0, ranges, fill, 0)
    homes = [owner_ref[me, r] // REQ_INST for r in range(ranges)]
    pick = jnp.zeros(pick_ref.shape, f32)
    put = jnp.zeros(put_ref.shape, f32)
    for r in range(ranges):
        rank = sum([(homes[e] == homes[r]).astype(jnp.int32) for e in range(r)], jnp.int32(0))
        slot = homes[r] * CAP + rank
        pick = jnp.where((iota(pick.shape, 0) == r) & (iota(pick.shape, 1) == slot), 1.0, pick)
        put = jnp.where((iota(put.shape, 1) == r) & (iota(put.shape, 0) == slot), 1.0, put)
    pick_ref[...] = pick
    put_ref[...] = put


def pick_ranges(groups, pick_ref, got_ref, out_ref, stage):
    slots = got_ref.shape[0] // groups
    stage[...] = got_ref[...].astype(f32)
    pick = pick_ref[...]
    for g in range(groups):
        value = stage[pl.ds(g, slots, stride=groups), :]
        out_ref[:, g * HEAD_DIM : (g + 1) * HEAD_DIM] = jnp.dot(
            pick, value, preferred_element_type=f32
        ).astype(bf16)


def place_before(shift):
    return (lax.axis_index("tp") // SIDE + SIDE - shift) % SIDE


def spread_queries(groups, chunks, qf, base):
    ranges = chunks[0].shape[0]
    for k, chunk in zip((0,) + SHIFTS, chunks):
        x = (lax.axis_index("tp") + SIDE - k) % SIDE
        at = pl.multiple_of(x * (groups * ranges) + base, groups * ranges)
        for g in range(groups):
            cols = slice(g * HEAD_DIM, (g + 1) * HEAD_DIM)
            qf[pl.ds(at + g * ranges, ranges), :] = chunk[:, cols].astype(f32)


def attend_row(groups, ranges, plan, k_ref, v_ref, wait_k, wait_v, out_ref, qf, base, of, lf):
    rows = SIDE * groups
    half = rows // 2
    pages, slice_tokens, pair = k_ref.shape
    scale = 1.0 / math.sqrt(HEAD_DIM)
    exp2_scale = scale * math.log2(math.e)
    top = iota((rows, HEAD_DIM), 0) < half

    def load(ref, page, span):
        return ref[pl.ds(page, span)].reshape(span * slice_tokens, pair)

    def scores(span, r, page, low, high):
        q = qf[pl.ds(base + r, rows, stride=ranges), :]
        zero = jnp.zeros_like(q)
        wide = jnp.concatenate(
            [jnp.where(top, q, zero), jnp.where(top, zero, q)], axis=1
        ).astype(bf16)
        k = load(k_ref, page, span)
        s = lax.dot_general(wide, k, (((1,), (1,)), ((), ())), preferred_element_type=f32)
        at = iota((1, span * slice_tokens), 1) + page * slice_tokens
        return s + jnp.where((at >= low) & (at < high), 0.0, VERY_LOW)

    def softmax(s):
        m = jnp.maximum(jnp.max(s, axis=1, keepdims=True), FLOOR)
        p = jnp.exp2((s - m) * exp2_scale)
        total = jnp.sum(p, axis=1, keepdims=True)
        some = total > 0.0
        safe = jnp.where(some, total, 1.0)
        lse = jnp.where(some, m * scale + jnp.log(safe), VERY_LOW)
        return p.astype(bf16), 1.0 / safe, jnp.broadcast_to(lse, (rows, HEAD_DIM))

    def values(span, page, p, inverse):
        o = jnp.dot(p, load(v_ref, page, span), preferred_element_type=f32)
        return jnp.where(top, o[:, :HEAD_DIM], o[:, HEAD_DIM:]) * inverse

    def place(r):
        return pl.ds(pl.multiple_of(r * rows, 8), rows)

    def later(e):
        return plan[RANGE_ROW, e], plan[PAGE_ROW, e], plan[LOW_ROW, e], plan[HIGH_ROW, e]

    def join(r, o, lse):
        at = place(r)
        old = lf[at, :]
        high = jnp.maximum(old, lse)
        share_old = jnp.exp(old - high)
        share = jnp.exp(lse - high)
        total = share_old + share
        of[at, :] = (of[at, :] * share_old + o * share) / total
        lf[at, :] = high + jnp.log(total)

    work = []
    for r in range(ranges):
        start = plan[START_ROW, r]
        page = jnp.minimum(start, pages - FIRST)
        work.append((FIRST, r, page, start * slice_tokens, plan[END_ROW, r]))
    for e in range(MORE):
        work.append((CHUNK, *later(e)))
    wait_k()
    parts = [scores(*w) for w in work]
    parts = [softmax(one) for one in parts]
    wait_v()
    outs = [values(w[0], w[2], p[0], p[1]) for p, w in zip(parts, work)]

    for w, (_, _, lse), o in zip(work[:ranges], parts, outs):
        of[place(w[1]), :] = o
        lf[place(w[1]), :] = lse
    for w, (_, _, lse), o in zip(work[ranges:], parts[ranges:], outs[ranges:]):
        join(w[1], o, lse)

    def few(b, carry):
        work = [later(MORE + b * FEW + j) for j in range(FEW)]
        parts = [softmax(scores(CHUNK, *w)) for w in work]
        outs = [values(CHUNK, w[1], p[0], p[1]) for p, w in zip(parts, work)]
        for w, (_, _, lse), o in zip(work, parts, outs):
            join(w[0], o, lse)
        return carry

    lax.fori_loop(0, (jnp.maximum(plan[COUNT_ROW, 0] - MORE, 0) + FEW - 1) // FEW, few, 0)

    lanes = iota((ranges, HEAD_DIM), 1)
    for x in range(SIDE):
        lse = jnp.zeros((ranges, HEAD_DIM), f32)
        for g in range(groups):
            at = pl.ds(x * groups + g, ranges, stride=rows)
            out_ref[x, :, g * HEAD_DIM : (g + 1) * HEAD_DIM] = of[at, :].astype(bf16)
            mine = (lanes == g) | (lanes == g + groups) | (lanes == g + 2 * groups)
            lse = jnp.where(mine, lf[at, :], lse)
        out_ref[x, :, groups * HEAD_DIM :] = split3(lse, lanes, groups)


def cache_copies(cache, target, shift, sems, first):
    pair = target.shape[-1]
    y = place_before(shift)
    columns = pl.ds(pl.multiple_of(y * pair, pair), pair)
    return [
        pltpu.make_async_copy(cache.at[:, w, :, columns], target.at[w], sems.at[first + w])
        for w in range(2)
    ]


def row_copy(row, held, shift, sem):
    y = place_before(shift)
    return pltpu.make_async_copy(row, held.at[pl.ds(y * SIDE, SIDE)], sem)


def attend_own(groups, plan_hbm, block, cache, held, plan, chunks, kv, row, qf, of, lf, sems):
    rows = cache_copies(cache, kv, 0, sems, 0)
    small = [pltpu.make_async_copy(plan_hbm, plan, sems.at[2])]
    small.append(pltpu.make_async_copy(block, chunks, sems.at[3]))
    for copy in small + rows:
        copy.start()
    for copy in small:
        copy.wait()
    spread_queries(groups, [chunks.at[i] for i in range(SIDE)], qf, 0)
    attend_row(
        groups, block.shape[1], plan, kv.at[0], kv.at[1], rows[0].wait, rows[1].wait, row, qf, 0, of, lf
    )
    out = row_copy(row, held, 0, sems.at[4])
    out.start()
    out.wait()


def attend_others(groups, shifts, plan_hbm, *refs):
    count = len(shifts)
    given = refs[:count]
    cache, held_in, held, plan, blocks, kv, row, qf, of, lf, sems = refs[count:]
    ranges = given[0].shape[1]
    size = SIDE * groups * ranges
    small = [pltpu.make_async_copy(plan_hbm, plan, sems.at[0])]
    for i, block in enumerate(given):
        small.append(pltpu.make_async_copy(block, blocks.at[i], sems.at[1 + i]))
    rows = [
        cache_copies(cache, kv.at[i], k, sems, 1 + count + 2 * i) for i, k in enumerate(shifts)
    ]
    for copy in small + rows[0]:
        copy.start()
    for copy in small:
        copy.wait()
    for i in range(count):
        spread_queries(groups, [blocks.at[i, j] for j in range(SIDE)], qf, i * size)
    out = 1 + 3 * count

    def one(i, carry):
        def wait(w):
            for k in range(count):

                @pl.when(i == k)
                def _():
                    rows[k][w].wait()
                    if w == 0 and k + 1 < count:
                        for copy in rows[k + 1]:
                            copy.start()

        wait_k, wait_v = functools.partial(wait, 0), functools.partial(wait, 1)
        keys, values = kv.at[i, 0], kv.at[i, 1]
        base = pl.multiple_of(i * size, size)
        attend_row(groups, ranges, plan, keys, values, wait_k, wait_v, row.at[i], qf, base, of, lf)
        shift = jnp.where(i == 0, shifts[0], shifts[-1])
        row_copy(row.at[i], held, shift, sems.at[out + i]).start()
        return carry

    lax.fori_loop(0, count, one, 0)
    for i, shift in enumerate(shifts):
        row_copy(row.at[i], held, shift, sems.at[out + i]).wait()


def merge_sources(groups, put_ref, in_ref, out_ref, stage):
    sources, ranges = in_ref.shape[0], in_ref.shape[1]
    slots = out_ref.shape[0] // PAD
    lane = iota((ranges, HEAD_DIM), 1)
    lses = [join3(in_ref[i, :, groups * HEAD_DIM :], groups) for i in range(sources)]
    top = functools.reduce(jnp.maximum, lses)
    shares = [jnp.exp(l - top) for l in lses]
    total = functools.reduce(jnp.add, shares)
    lse = top + jnp.log(total)
    inverse = 1.0 / total
    shares = [s * inverse for s in shares]
    put = put_ref[...].astype(bf16)
    for g in range(groups):
        cols = slice(g * HEAD_DIM, (g + 1) * HEAD_DIM)
        acc = jnp.zeros((ranges, HEAD_DIM), f32)
        for i in range(sources):
            acc = acc + shares[i][:, g : g + 1] * in_ref[i, :, cols].astype(f32)
        stage[pl.ds(g, slots, stride=PAD), :] = jnp.dot(
            put, acc.astype(bf16), preferred_element_type=f32
        )
    second, third = pltpu.roll(lse, groups, 1), pltpu.roll(lse, 2 * groups, 1)
    stats = jnp.where(lane < groups, lse, jnp.where(lane < 2 * groups, second, third))
    parts = split3(stats, lane, groups)
    stage[pl.ds(groups, slots, stride=PAD), :] = jnp.dot(put, parts, preferred_element_type=f32)
    for g in range(groups + 1, PAD):
        stage[pl.ds(g, slots, stride=PAD), :] = jnp.zeros((slots, HEAD_DIM), f32)
    out_ref[...] = stage[...].astype(bf16)


def finish(steps, heads, in_ref, owner_ref, q_ref, k_ref, v_ref, out_ref, stage):
    groups = steps * heads
    lenders = in_ref.shape[0] // (CAP * PAD)
    scale = 1.0 / math.sqrt(HEAD_DIM)
    stage[...] = in_ref[...].astype(f32)

    def group(g):
        return jnp.concatenate(
            [stage[pl.ds(c * PAD + g, lenders, stride=CAP * PAD), :] for c in range(CAP)], axis=0
        )

    lses = jnp.transpose(join3(group(groups), groups), (1, 0))
    owned = owner_ref[...].astype(jnp.int32) == iota(owner_ref.shape, 0)
    keys = [k_ref[t].astype(f32) for t in range(steps)]
    values = [v_ref[t].astype(f32) for t in range(steps)]
    for s in range(steps):
        for h in range(heads):
            g = s * heads + h
            cols = slice(h * HEAD_DIM, (h + 1) * HEAD_DIM)
            q = q_ref[s, :, cols].astype(f32)
            scores = [
                jnp.sum(q * keys[t], axis=1, keepdims=True) * scale for t in range(s + 1)
            ]
            lent = jnp.where(owned, jnp.broadcast_to(lses[g : g + 1, :], owned.shape), VERY_LOW)
            top = functools.reduce(jnp.maximum, scores)
            top = jnp.maximum(top, jnp.max(lent, axis=1, keepdims=True))
            share = jnp.where(owned, jnp.exp(lent - top), 0.0)
            total = jnp.sum(share, axis=1, keepdims=True)
            high = share.astype(bf16).astype(f32)
            parts = jnp.concatenate([high, share - high], axis=0).astype(bf16)
            sums = jnp.dot(parts, group(g).astype(bf16), preferred_element_type=f32)
            acc = sums[: len(share)] + sums[len(share) :]
            for t in range(s + 1):
                weight = jnp.exp(scores[t] - top)
                total = total + weight
                acc = acc + weight.astype(bf16).astype(f32) * values[t]
            out_ref[s, :, cols] = (acc / total).astype(bf16)


def x_shift(k):
    return [(SIDE * y + x, SIDE * y + (x + k) % SIDE) for y in range(SIDE) for x in range(SIDE)]


def y_shift(k):
    return [(SIDE * y + x, SIDE * ((y + k) % SIDE) + x) for y in range(SIDE) for x in range(SIDE)]


def on_device(queries, new_kv, page_cache, range_owner, range_start, range_tokens):
    steps, requests, columns = queries.shape
    lenders = lax.axis_size("inst")
    tp_count = lax.axis_size("tp")
    my_tp = lax.axis_index("tp")
    pages, _, slice_tokens, kv_columns = page_cache.shape
    ranges = range_owner.shape[1]
    heads = columns // HEAD_DIM
    groups = steps * heads
    kv_heads = kv_columns // HEAD_DIM
    group_size = heads * tp_count // kv_heads
    slots = lenders * CAP
    wide = (groups + 1) * HEAD_DIM
    vmem = pl.BlockSpec(memory_space=pltpu.VMEM)
    smem = pl.BlockSpec(memory_space=pltpu.SMEM)
    hbm = pl.BlockSpec(memory_space=pltpu.HBM)
    params = pltpu.CompilerParams(vmem_limit_bytes=24 * 2**20)
    grant = pltpu.CompilerParams(vmem_limit_bytes=57 * 2**20)
    whole = pltpu.CompilerParams(vmem_limit_bytes=64 * 2**20 - 2**17)
    dma = pltpu.SemaphoreType.DMA

    sent, slot_owner = pl.pallas_call(
        prepare,
        in_specs=[hbm] * 2,
        out_specs=[vmem] * 2,
        out_shape=[
            jax.ShapeDtypeStruct((slots * groups, HEAD_DIM), bf16),
            jax.ShapeDtypeStruct((requests, slots), f32),
        ],
        scratch_shapes=[
            pltpu.VMEM(queries.shape, bf16),
            pltpu.VMEM(range_owner.shape, jnp.int32),
            pltpu.VMEM((slots * groups, HEAD_DIM), f32),
            dma((2,)),
        ],
        compiler_params=whole,
        name="prepare",
    )(queries, range_owner)
    got = lax.all_to_all(sent, "inst", split_axis=0, concat_axis=0, tiled=True)

    plan, pick, put = pl.pallas_call(
        functools.partial(make_plan, slice_tokens, pages),
        in_specs=[smem] * 3,
        out_specs=[smem, vmem, vmem],
        out_shape=[
            jax.ShapeDtypeStruct((8, ranges), jnp.int32),
            jax.ShapeDtypeStruct((ranges, slots), f32),
            jax.ShapeDtypeStruct((slots, ranges), f32),
        ],
        compiler_params=params,
        name="make_plan",
    )(range_owner, range_start, range_tokens)
    head = my_tp * heads // group_size
    fresh = lax.dynamic_slice_in_dim(new_kv, head * HEAD_DIM, HEAD_DIM, axis=3)

    own = pl.pallas_call(
        functools.partial(pick_ranges, groups),
        in_specs=[vmem] * 2,
        out_specs=vmem,
        out_shape=jax.ShapeDtypeStruct((ranges, groups * HEAD_DIM), bf16),
        scratch_shapes=[pltpu.VMEM((slots * groups, HEAD_DIM), f32)],
        compiler_params=params,
        name="pick_ranges",
    )(pick, got)
    before, after = (lax.ppermute(own, "tp", x_shift(k)) for k in (1, SIDE - 1))
    block = jnp.stack([own, before, after, lax.ppermute(before, "tp", x_shift(1))])
    near = {k: lax.ppermute(block, "tp", y_shift(k)) for k in (1, SIDE - 1)}

    pair = 2 * HEAD_DIM
    size = SIDE * groups * ranges
    partial_type = jax.ShapeDtypeStruct((tp_count, ranges, wide), bf16)
    plan_type = pltpu.SMEM(plan.shape, jnp.int32)
    row_scratch = [pltpu.VMEM((size, HEAD_DIM), f32)] * 2
    partial = pl.pallas_call(
        functools.partial(attend_own, groups),
        in_specs=[hbm] * 3,
        out_specs=hbm,
        out_shape=partial_type,
        scratch_shapes=[
            plan_type,
            pltpu.VMEM((SIDE, ranges, groups * HEAD_DIM), bf16),
            pltpu.VMEM((2, pages, slice_tokens, pair), bf16),
            pltpu.VMEM((SIDE, ranges, wide), bf16),
            pltpu.VMEM((size + ranges, HEAD_DIM), f32),
        ]
        + row_scratch
        + [dma((5,))],
        compiler_params=grant,
        cost_estimate=pl.CostEstimate(flops=10**9, bytes_accessed=2**23, transcendentals=0),
        name="attend_own",
    )(plan, block, page_cache)
    passed, partial = lax.optimization_barrier((near[1], partial))
    far = lax.ppermute(passed, "tp", y_shift(1))
    for given in ({1: passed, SIDE - 1: near[SIDE - 1]}, {2: far}):
        count = len(given)
        partial = pl.pallas_call(
            functools.partial(attend_others, groups, list(given)),
            in_specs=[hbm] * (count + 3),
            out_specs=hbm,
            out_shape=partial_type,
            scratch_shapes=[
                plan_type,
                pltpu.VMEM((count, SIDE, ranges, groups * HEAD_DIM), bf16),
                pltpu.VMEM((count, 2, pages, slice_tokens, pair), bf16),
                pltpu.VMEM((count, SIDE, ranges, wide), bf16),
                pltpu.VMEM((count * size + ranges, HEAD_DIM), f32),
            ]
            + row_scratch
            + [dma((1 + 4 * count,))],
            input_output_aliases={count + 2: 0},
            compiler_params=whole,
            cost_estimate=pl.CostEstimate(
                flops=count * 10**9, bytes_accessed=count * 2**22, transcendentals=0
            ),
            name="attend_others",
        )(plan, *given.values(), page_cache, partial)

    parts = lax.all_to_all(partial, "tp", split_axis=0, concat_axis=0, tiled=True)
    lent = pl.pallas_call(
        functools.partial(merge_sources, groups),
        in_specs=[vmem] * 2,
        out_specs=vmem,
        out_shape=jax.ShapeDtypeStruct((slots * PAD, HEAD_DIM), bf16),
        scratch_shapes=[pltpu.VMEM((slots * PAD, HEAD_DIM), f32)],
        compiler_params=params,
        name="merge_sources",
    )(put, parts)
    back = lax.all_to_all(lent, "inst", split_axis=0, concat_axis=0, tiled=True)
    return pl.pallas_call(
        functools.partial(finish, steps, heads),
        in_specs=[vmem] * 5,
        out_specs=vmem,
        out_shape=jax.ShapeDtypeStruct((steps, requests, columns), bf16),
        scratch_shapes=[pltpu.VMEM((slots * PAD, HEAD_DIM), f32)],
        compiler_params=params,
        name="finish",
    )(back, slot_owner, queries, fresh[:, :, 0], fresh[:, :, 1])


def solution(mesh):
    placed = (
        P(None, "inst", "tp"),
        P(None, "inst", None, None),
        P("inst", None, "tp", None),
        P(),
        P(),
        P(),
    )
    return jax.shard_map(
        on_device, mesh=mesh, in_specs=placed, out_specs=P(None, "inst", "tp"), check_vma=False
    )
```
